32 devices in a mesh: seq: 8 (over z, core), blk: 4 (over y, x).
Axes of the slice: x: 2, y: 2, z: 4, core: 2. Of those that a mesh axis runs over, the one named last changes fastest.
Arguments:
- tokens: bfloat16 [4096, 3072], P(('seq', 'blk')), may hold values from -8.6 to 8.6
- project_weight: bfloat16 [3, 3072, 2048], P(None, None, 'seq')
- noisy_latent: float32 [4096, 64], P(('seq', 'blk')), may hold values from -6 to 6
- final_weight: bfloat16 [2048, 64], replicated, may hold values from -0.5 to 0.5
- conv_weight: bfloat16 [432, 512], replicated, may hold values from -0.3125 to 0.3125
- norm_gain: float32 [512], replicated, may hold values from 0.1 to 1.9
- norm_shift: float32 [512], replicated, may hold values from -3 to 3
- owner_count: int32 [32], replicated, may hold values from 1 to 4, 64 in all
- intersection: int32 [64, 4], replicated, may hold values from 0 to 31, as said below
Outputs:
- decoded: bfloat16 [32, 4, 512, 2048], P(('seq', 'blk'))
The draws below stay inside these ranges and needn't reach their ends.
Inputs may be any that keep to these rules, and one draw needn't show every extreme that they name: Owner o holds pixel tiles s to s + owner_count[o] - 1, s the sum of the counts below o; the counts sum to 64 and one owner holds exactly 4. `intersection`: row p names the four latent tiles of a 2 x 2 block of neighbouring tiles on a grid of 8 rows by 4 columns, tile r * 4 + c at row r, column c, in the order top left, top right, bottom left, bottom right.
All inputs are finite; a program needn't handle non-finite values.
Results may differ from the reference program's by a relative error of at most 0.014.
Values may be sent and summed in bfloat16 or wider, within the bound.
A program may use at most 128 MiB of HBM per device.

```python
import math
import jax
import jax.numpy as jnp
import numpy as np
from jax import lax

D = 3072
HEAD_DIM = 128
HEADS = 16
LATENT_CH = 16
CH = 512
GROUPS = 32
TILE_F = 2
TILE_PH = 8
TILE_PW = 8
MAXPIX = 4
TOKENS = 4096
PATCH_CH = 64
PIXEL_TILES = 64
TILE_ROWS = 8
TILE_COLS = 4
DEVICES = 32


def draw_tokens(key, part):
    key = jax.random.fold_in(key, 11)
    base_key = jax.random.fold_in(key, 0)
    return jnp.clip(jax.random.normal(base_key, (TOKENS, D), jnp.float32), -6.0, 6.0).astype(jnp.bfloat16)


def draw_project_weight(key, part):
    key = jax.random.fold_in(key, 23)
    first_key, second_key, third_key = jax.random.split(key, 3)
    matrix_shape = (D, HEADS * HEAD_DIM)
    spread = D ** (-0.5)
    query_part = jnp.clip(jax.random.normal(first_key, matrix_shape, jnp.float32), -6.0, 6.0) * (2.0 * spread)
    key_part = jnp.clip(jax.random.normal(second_key, matrix_shape, jnp.float32), -6.0, 6.0) * (2.0 * spread)
    value_part = jnp.clip(jax.random.normal(third_key, matrix_shape, jnp.float32), -6.0, 6.0) * spread
    return jnp.stack([query_part, key_part, value_part]).astype(jnp.bfloat16)


def draw_intersection(key, part):
    key = jax.random.fold_in(key, 37)
    row_key, column_key = jax.random.split(key)
    anchor_row = jax.random.randint(row_key, (PIXEL_TILES,), 0, TILE_ROWS - 1)
    anchor_col = jax.random.randint(column_key, (PIXEL_TILES,), 0, TILE_COLS - 1)
    anchor_row = anchor_row.at[0].set(0).at[PIXEL_TILES - 1].set(TILE_ROWS - 2)
    anchor_col = anchor_col.at[0].set(0).at[PIXEL_TILES - 1].set(TILE_COLS - 2)
    corner = anchor_row * TILE_COLS + anchor_col
    return jnp.stack([corner, corner + 1, corner + TILE_COLS, corner + TILE_COLS + 1], axis=1).astype(jnp.int32)


def shard_levels(stream_key, shape, shards, low, top_value):
    def one(position, parts):
        heights = jax.random.uniform(jax.random.fold_in(jax.random.fold_in(stream_key, 6), position), (parts,), jnp.float32, low / len(shards), top_value / len(shards))
        return jnp.repeat(jnp.exp(heights), shape[position] // parts).reshape((-1,) + (1,) * (len(shape) - position - 1))

    loudness = one(*shards[0])
    for cut in shards[1:]:
        loudness = loudness * one(*cut)
    return loudness


def length_profile(number_of, total, most, lean):
    portions = [(1 << 20) // math.isqrt(rank ** lean) + 1 for rank in range(2, number_of + 1)]
    rest, holding = total - most - (number_of - 1), [1] * (number_of - 1)
    while rest > 0:
        movable = [i for i in range(number_of - 1) if holding[i] < most]
        pool, remaining = sum([portions[i] for i in movable]), rest
        for i in movable:
            more = min(most - holding[i], max(1, remaining * portions[i] // pool), rest)
            holding[i] = holding[i] + more
            rest = rest - more
    return np.array([most] + holding)


def uneven(own_key, amount, total, bound, skew):
    if amount == 2:
        one = jax.random.randint(own_key, (), max(1, total - bound), min(bound, total - 1) + 1)
        return jnp.stack([one, total - one])
    tallies = jnp.asarray(length_profile(amount, total, bound, skew), jnp.int32)
    twos = (amount - 1) // 2
    donor, taker = tallies[1:1 + 2 * twos:2], tallies[2:2 + 2 * twos:2]
    margin = jnp.minimum(donor - 1, bound - taker)
    moved = jax.random.randint(jax.random.fold_in(own_key, 1), (twos,), 0, 1 << 20) % (margin + 1)
    tallies = tallies.at[1:1 + 2 * twos:2].set(donor - moved).at[2:2 + 2 * twos:2].set(taker + moved)
    return tallies[jax.random.permutation(jax.random.fold_in(own_key, 2), amount)]


def gaussian(own_key, dims, scale, limit, cuts=(), held_as=jnp.bfloat16):
    level = shard_levels(own_key, dims, cuts, -0.22, 0.18) if cuts else 1.0
    array = jax.random.normal(own_key, dims, jnp.float32) * scale * level
    return jnp.minimum(jnp.maximum(array, -limit), limit).astype(held_as)


def setup_inputs(seed: int = 0) -> dict:
    key_list = jax.random.split(jax.random.key(seed), 10)
    return {
        "tokens": draw_tokens(jax.random.fold_in(key_list[9], 71), 0),
        "project_weight": draw_project_weight(jax.random.fold_in(key_list[9], 71), 0),
        "noisy_latent": gaussian(key_list[2], (TOKENS, PATCH_CH), 1.0, 6.0, ((0, 32),), jnp.float32),
        "final_weight": gaussian(key_list[3], (HEADS * HEAD_DIM, PATCH_CH), (HEADS * HEAD_DIM // 16) ** -0.5, 0.5),
        "conv_weight": gaussian(key_list[4], (27 * LATENT_CH, CH), (27 * LATENT_CH) ** -0.5, 0.3125),
        "norm_gain": jnp.clip(1.0 + 0.18 * jax.random.normal(key_list[5], (CH,), jnp.float32), 0.1, 1.9),
        "norm_shift": gaussian(key_list[6], (CH,), 0.5, 3.0, (), jnp.float32),
        "owner_count": uneven(key_list[7], DEVICES, PIXEL_TILES, MAXPIX, 2).astype(jnp.int32),
        "intersection": draw_intersection(jax.random.fold_in(key_list[9], 71), 0),
    }


scale_factor = 0.476986
step_size = 0.25
norm_eps = 1e-06

def decode_tile(all_tiles, tile_ids, conv_weight, norm_gain, norm_shift):
    pieces = all_tiles[tile_ids]
    upper = jnp.concatenate([pieces[0], pieces[1]], axis=3)
    lower = jnp.concatenate([pieces[2], pieces[3]], axis=3)
    region = jnp.concatenate([upper, lower], axis=2)
    padded = jnp.pad(region, ((0, 0), (2, 0), (1, 1), (1, 1)), mode='edge')
    frames = region.shape[1]
    height = region.shape[2]
    breadth = region.shape[3]
    tap_list = []
    for tap_time in range(3):
        for tap_row in range(3):
            for tap_col in range(3):
                window = padded[:, tap_time:tap_time + frames, tap_row:tap_row + height, tap_col:tap_col + breadth]
                tap_list.append(window.reshape(region.shape[0], -1))
    patches = jnp.concatenate(tap_list, axis=0)
    convolved = lax.dot_general(conv_weight, patches, (((0,), (0,)), ((), ())), preferred_element_type=jnp.float32)
    channels = convolved.shape[0]
    grouped = convolved.reshape(GROUPS, channels // GROUPS, -1)
    group_mean = lax.optimization_barrier(jnp.mean(grouped, axis=(1, 2), keepdims=True))
    group_var = lax.optimization_barrier(jnp.mean(jnp.square(grouped - group_mean), axis=(1, 2), keepdims=True))
    normed = ((grouped - group_mean) * lax.rsqrt(group_var + norm_eps)).reshape(channels, -1)
    normed = normed * norm_gain[:, None] + norm_shift[:, None]
    return jax.nn.silu(normed).astype(jnp.bfloat16)

def attend_head(head_data):
    queries, key_rows, value_rows = head_data
    query_block = min(2048, queries.shape[0])
    blocks = queries.reshape(-1, query_block, queries.shape[1])
    inv_root = queries.shape[1] ** (-0.5)

    def one_block(query_rows):
        scores = jnp.dot(query_rows, key_rows.T, preferred_element_type=jnp.float32) * inv_root
        row_max = lax.optimization_barrier(jnp.max(scores, axis=1, keepdims=True))
        exp_scores = jnp.exp(scores - row_max)
        denominator = lax.optimization_barrier(jnp.sum(exp_scores, axis=1, keepdims=True))
        numerator = jnp.dot(exp_scores.astype(jnp.bfloat16), value_rows, preferred_element_type=jnp.float32)
        return (numerator / denominator).astype(jnp.bfloat16)
    return lax.map(one_block, blocks).reshape(queries.shape)

def reference(tokens, project_weight, noisy_latent, final_weight, conv_weight, norm_gain, norm_shift, owner_count, intersection):
    projected = []
    for proj_index in range(3):
        product = jnp.dot(tokens, project_weight[proj_index], preferred_element_type=jnp.float32).astype(jnp.bfloat16)
        projected.append(product.reshape(TOKENS, HEADS, HEAD_DIM).transpose(1, 0, 2))
    attended = lax.map(attend_head, (projected[0], projected[1], projected[2]))
    attended = attended.transpose(1, 0, 2).reshape(TOKENS, HEADS * HEAD_DIM)
    velocity = jnp.dot(attended, final_weight, preferred_element_type=jnp.float32)
    latent = (noisy_latent - step_size * velocity) / scale_factor
    tiles = latent.reshape(DEVICES, TILE_F, TILE_PH, TILE_PW, LATENT_CH, 2, 2).transpose(0, 4, 1, 2, 5, 3, 6)
    tiles = tiles.reshape(DEVICES, LATENT_CH, TILE_F, 2 * TILE_PH, 2 * TILE_PW).astype(jnp.bfloat16)
    pixel = lax.map(lambda tile_ids: decode_tile(tiles, tile_ids, conv_weight, norm_gain, norm_shift), intersection)
    count_ends = jnp.cumsum(owner_count, dtype=jnp.int32)
    first_tile = count_ends - owner_count
    slot_range = jnp.arange(MAXPIX, dtype=jnp.int32)
    slot_tiles = jnp.minimum(first_tile[:, None] + slot_range[None, :], PIXEL_TILES - 1).astype(jnp.int32)
    occupied = slot_range[None, :] < owner_count[:, None]
    picked = pixel[slot_tiles]
    return jnp.where(occupied[:, :, None, None], picked, jnp.zeros((), jnp.bfloat16))
```

```python
import functools
import math

import jax
import jax.numpy as jnp
from jax import lax
from jax.experimental import pallas as pl
from jax.experimental.pallas import tpu as pltpu
from jax.sharding import PartitionSpec as P

HEAD_DIM = 128
LATENT_CH = 16
GROUPS = 32
TILE_F = 2
TILE_PH = 8
TILE_PW = 8
MAXPIX = 4

scale_factor = 0.476986
step_size = 0.25
norm_eps = 1e-06

MESH = pl.DeviceIdType.MESH
F32 = jnp.float32
BF16 = jnp.bfloat16
TILE_VOX = TILE_F * 4 * TILE_PH * TILE_PW


def nt_dot(a, b):
    return lax.dot_general(a, b, (((1,), (1,)), ((), ())), preferred_element_type=F32)


def attention_kernel(
    chain,
    n_blk,
    tokens_ref,
    weight_ref,
    noisy_ref,
    final_ref,
    tiles_ref,
    tok,
    weight,
    q_all,
    kv_all,
    acc_all,
    max_all,
    vel_out,
    vel_in,
    own_tile,
    spread,
    local_sem,
    tok_send,
    tok_recv,
    kv_send,
    kv_recv,
    vel_send,
    vel_recv,
    tile_send,
    tile_recv,
    sib_send,
    sib_recv,
):
    n_seq = 2 * chain
    seq = lax.axis_index("seq")
    blk = lax.axis_index("blk")
    z = lax.div(seq, 2)
    core = lax.rem(seq, 2)
    me = seq * n_blk + blk
    rows = tokens_ref.shape[0]
    pair = 2 * rows
    width = q_all.shape[2]
    heads = width // HEAD_DIM

    load_weight = pltpu.make_async_copy(weight_ref, weight, local_sem.at[0])
    load_weight.start()
    load_tokens = pltpu.make_async_copy(tokens_ref, tok.at[z, core], local_sem.at[1])
    load_tokens.start()

    barrier = pltpu.get_barrier_semaphore()

    def greet(step, carry):
        other = lax.rem(me + step, n_seq * n_blk)
        pl.semaphore_signal(
            barrier,
            inc=1,
            device_id=(lax.div(other, n_blk), lax.rem(other, n_blk)),
            device_id_type=MESH,
        )
        return carry

    lax.fori_loop(1, n_seq * n_blk, greet, 0)
    pl.semaphore_wait(barrier, n_seq * n_blk - 1)

    def tok_copy(origin, side, target_z, target_core):
        source = tokens_ref if origin is None else tok.at[origin, core]
        origin = z if origin is None else origin
        return pltpu.make_async_remote_copy(
            src_ref=source,
            dst_ref=tok.at[origin, core],
            send_sem=tok_send.at[origin, side],
            recv_sem=tok_recv.at[origin, core],
            device_id=(target_z * 2 + target_core, blk),
            device_id_type=MESH,
        )

    def tok_arrival(origin, origin_core):
        pltpu.make_async_remote_copy(
            src_ref=tok.at[origin, origin_core],
            dst_ref=tok.at[origin, origin_core],
            send_sem=tok_send.at[origin, 0],
            recv_sem=tok_recv.at[origin, origin_core],
            device_id=(z * 2 + 1 - core, blk),
            device_id_type=MESH,
        ).wait_recv()

    def go_left(origin):
        return tok_copy(origin, 0, z - 1, core)

    def go_right(origin):
        return tok_copy(origin, 1, z + 1, core)

    def go_over(origin):
        return tok_copy(origin, 2, z, 1 - core)

    def kv_copy(origin, hop):
        place = kv_all.at[origin, :, pl.ds(pl.multiple_of(blk * pair, pair), pair), :]
        return pltpu.make_async_remote_copy(
            src_ref=place,
            dst_ref=place,
            send_sem=kv_send.at[origin, hop],
            recv_sem=kv_recv.at[origin, blk],
            device_id=(seq, lax.rem(blk + hop, n_blk)),
            device_id_type=MESH,
        )

    def kv_arrival(origin, hop):
        source = lax.rem(blk + n_blk - hop, n_blk)
        place = kv_all.at[origin, :, pl.ds(pl.multiple_of(source * pair, pair), pair), :]
        pltpu.make_async_remote_copy(
            src_ref=place,
            dst_ref=place,
            send_sem=kv_send.at[origin, hop],
            recv_sem=kv_recv.at[origin, source],
            device_id=(seq, lax.rem(blk + hop, n_blk)),
            device_id_type=MESH,
        ).wait_recv()

    def project(origin):
        x = tok[origin].reshape(pair, tok.shape[3])
        query = jnp.dot(x, weight[0], preferred_element_type=F32)
        q_all[origin] = (query * (HEAD_DIM**-0.5 * math.log2(math.e))).astype(BF16)
        place = pl.ds(pl.multiple_of(blk * pair, pair), pair)
        for part in range(2):
            kv_all[origin, part, place, :] = jnp.dot(
                x, weight[part + 1], preferred_element_type=F32
            ).astype(BF16)
        for hop in range(1, n_blk):
            kv_copy(origin, hop).start()
        for head in range(heads):
            max_all[origin, head] = jnp.full((pair, HEAD_DIM), -1e30, F32)
            acc_all[origin, head] = jnp.zeros((pair, 2 * HEAD_DIM), F32)

    def attend(q_pair, kv_pair):
        for head in range(heads):
            lanes = pl.ds(head * HEAD_DIM, HEAD_DIM)
            scores = nt_dot(q_all[q_pair, :, lanes], kv_all[kv_pair, 0, :, lanes])
            old_max = max_all[q_pair, head]
            new_max = jnp.maximum(old_max, jnp.max(scores, axis=1, keepdims=True))
            rescale = jnp.exp2(old_max - new_max)
            weights = jnp.exp2(scores - new_max[:, :1]).astype(BF16)
            value = kv_all[kv_pair, 1, :, lanes]
            value = jnp.concatenate([value, jnp.ones_like(value)], axis=1)
            product = jnp.dot(weights, value, preferred_element_type=F32)
            acc_all[q_pair, head] = (
                acc_all[q_pair, head] * jnp.concatenate([rescale, rescale], axis=1) + product
            )
            max_all[q_pair, head] = new_max

    def each_of_step(step, action):
        if step >= chain:
            return
        if step == 0:
            action(z, None)
            return
        pl.when(z - step >= 0)(lambda: action(z - step, "left"))
        pl.when(z + step < chain)(lambda: action(z + step, "right"))

    def attend_range(q_pair, kv_pair, radius, over_queries):
        low = jnp.maximum(z - radius, 0)
        high = jnp.minimum(z + radius, chain - 1) + 1

        def one(index, carry):
            if over_queries:
                attend(index, kv_pair)
            else:
                attend(q_pair, index)
            return carry

        lax.fori_loop(low, high, one, 0)

    def forward(origin, side):
        tok_arrival(origin, core)
        if side == "left":
            pl.when(z < chain - 1)(lambda: go_right(origin).start())
        else:
            pl.when(z > 0)(lambda: go_left(origin).start())
        go_over(origin).start()

    def project_arrived(origin, side):
        tok_arrival(origin, 1 - core)
        project(origin)

    pl.when(z > 0)(lambda: go_left(None).start())
    pl.when(z < chain - 1)(lambda: go_right(None).start())
    go_over(None).start()

    token = lax.broadcasted_iota(jnp.int32, (rows, TILE_VOX), 0)
    voxel = lax.broadcasted_iota(jnp.int32, (rows, TILE_VOX), 1)
    row, column = (voxel >> 4) & 15, voxel & 15
    home = (voxel >> 8) * (TILE_PH * TILE_PW) + (row >> 1) * TILE_PW + (column >> 1)
    for sub in range(4):
        hit = (home == token) & ((row & 1) * 2 + (column & 1) == sub)
        spread[sub] = jnp.where(hit, 1.0, 0.0).astype(BF16)

    load_weight.wait()
    load_tokens.wait()
    project_arrived(z, None)

    for step in range(chain):
        each_of_step(step + 1, forward)
        each_of_step(step + 1, project_arrived)
        if step >= 1:
            each_of_step(step + 1, lambda o, side: attend_range(o, None, step - 1, False))

        def meet(origin, side):
            for hop in range(1, n_blk):
                kv_arrival(origin, hop)
            attend_range(None, origin, min(step + 1, chain - 1), True)

        each_of_step(step, meet)

    final = final_ref[pl.ds(pl.multiple_of(seq * width, width), width), :]

    def vel_copy(target_z, target_core):
        target = target_z * 2 + target_core
        return pltpu.make_async_remote_copy(
            src_ref=vel_out.at[target],
            dst_ref=vel_in.at[seq],
            send_sem=vel_send.at[target],
            recv_sem=vel_recv.at[seq],
            device_id=(target, blk),
            device_id_type=MESH,
        )

    for turn in range(chain):
        q_pair = lax.rem(z + 1 + turn, chain)
        attended = []
        for head in range(heads):
            total = acc_all[q_pair, head]
            attended.append((total[:, :HEAD_DIM] / total[:, HEAD_DIM:]).astype(BF16))
        part = jnp.dot(jnp.concatenate(attended, axis=1), final, preferred_element_type=F32)
        half = rows // 2
        for side in range(2):
            own = part[side * rows : (side + 1) * rows]
            vel_out[q_pair * 2 + side] = jnp.concatenate([own[:half], own[half:]], axis=1).astype(
                BF16
            )
        if turn < chain - 1:
            for side in range(2):
                vel_copy(q_pair, side).start()
        else:
            vel_copy(z, 1 - core).start()
    vel_in[seq] = vel_out[seq]

    def vel_arrival(hop, carry):
        source = lax.rem(seq + hop, n_seq)
        pltpu.make_async_remote_copy(
            src_ref=vel_out.at[source],
            dst_ref=vel_in.at[source],
            send_sem=vel_send.at[source],
            recv_sem=vel_recv.at[source],
            device_id=(source, blk),
            device_id_type=MESH,
        ).wait_recv()
        return carry

    lax.fori_loop(1, n_seq, vel_arrival, 0)
    packed = vel_in[0].astype(F32)
    for source in range(1, n_seq):
        packed = packed + vel_in[source].astype(F32)
    patch = noisy_ref.shape[1]
    velocity = jnp.concatenate([packed[:, :patch], packed[:, patch:]], axis=0)
    latent = ((noisy_ref[...] - step_size * velocity) / scale_factor).astype(BF16)
    channel = lax.broadcasted_iota(jnp.int32, (LATENT_CH, patch), 0)
    feature = lax.broadcasted_iota(jnp.int32, (LATENT_CH, patch), 1)
    tile = jnp.zeros((LATENT_CH, TILE_VOX), F32)
    for sub in range(4):
        pick = jnp.where(feature == channel * 4 + sub, 1.0, 0.0).astype(BF16)
        tile = tile + jnp.dot(
            nt_dot(pick, latent).astype(BF16), spread[sub], preferred_element_type=F32
        )
    own_tile[...] = tile.astype(BF16)

    n_same = chain * n_blk
    index = z * n_blk + blk
    keep = pltpu.make_async_copy(own_tile, tiles_ref.at[z, core, blk], local_sem.at[0])
    keep.start()

    def tile_copy(hop):
        other = lax.rem(index + hop, n_same)
        return pltpu.make_async_remote_copy(
            src_ref=own_tile,
            dst_ref=tiles_ref.at[z, core, blk],
            send_sem=tile_send.at[hop],
            recv_sem=tile_recv.at[index],
            device_id=(lax.div(other, n_blk) * 2 + core, lax.rem(other, n_blk)),
            device_id_type=MESH,
        )

    def tile_start(hop, carry):
        tile_copy(hop).start()
        return carry

    def tile_arrival(hop, carry):
        source = lax.rem(index + n_same - hop, n_same)
        pltpu.make_async_remote_copy(
            src_ref=own_tile,
            dst_ref=tiles_ref.at[lax.div(source, n_blk), core, lax.rem(source, n_blk)],
            send_sem=tile_send.at[hop],
            recv_sem=tile_recv.at[source],
            device_id=(lax.div(source, n_blk) * 2 + core, lax.rem(source, n_blk)),
            device_id_type=MESH,
        ).wait_recv()
        return carry

    lax.fori_loop(1, n_same, tile_start, 0)
    keep.wait()
    lax.fori_loop(1, n_same, tile_arrival, 0)
    over = pltpu.make_async_remote_copy(
        src_ref=tiles_ref.at[:, core],
        dst_ref=tiles_ref.at[:, core],
        send_sem=sib_send,
        recv_sem=sib_recv,
        device_id=(z * 2 + 1 - core, blk),
        device_id_type=MESH,
    )
    over.start()

    pl.when(z > 0)(lambda: go_left(None).wait_send())
    pl.when(z < chain - 1)(lambda: go_right(None).wait_send())
    go_over(None).wait_send()

    def settle(origin, side):
        if side == "left":
            pl.when(z < chain - 1)(lambda: go_right(origin).wait_send())
        else:
            pl.when(z > 0)(lambda: go_left(origin).wait_send())
        go_over(origin).wait_send()

    for step in range(1, chain):
        each_of_step(step, settle)

    def settle_kv(origin, carry):
        for hop in range(1, n_blk):
            kv_copy(origin, hop).wait_send()
        return carry

    lax.fori_loop(0, chain, settle_kv, 0)

    def settle_vel(hop, carry):
        other = lax.rem(seq + hop, n_seq)
        vel_copy(lax.div(other, 2), lax.rem(other, 2)).wait_send()
        return carry

    lax.fori_loop(1, n_seq, settle_vel, 0)

    def settle_tile(hop, carry):
        tile_copy(hop).wait_send()
        return carry

    lax.fori_loop(1, n_same, settle_tile, 0)
    over.wait_send()
    pltpu.make_async_remote_copy(
        src_ref=tiles_ref.at[:, 1 - core],
        dst_ref=tiles_ref.at[:, 1 - core],
        send_sem=sib_send,
        recv_sem=sib_recv,
        device_id=(z * 2 + 1 - core, blk),
        device_id_type=MESH,
    ).wait_recv()


def latent_tiles(n_seq, n_blk, tokens, project_weight, noisy_latent, final_weight):
    chain = n_seq // 2
    rows, depth = tokens.shape
    width = project_weight.shape[2]
    heads = width // HEAD_DIM
    pair = 2 * rows
    dma = pltpu.SemaphoreType.DMA
    vmem = pl.BlockSpec(memory_space=pltpu.VMEM)
    hbm = pl.BlockSpec(memory_space=pl.ANY)
    return pl.pallas_call(
        functools.partial(attention_kernel, chain, n_blk),
        out_shape=jax.ShapeDtypeStruct((chain, 2, n_blk, LATENT_CH, TILE_VOX), BF16),
        in_specs=[hbm, hbm, vmem, vmem],
        out_specs=hbm,
        scratch_shapes=[
            pltpu.VMEM((chain, 2, rows, depth), BF16),
            pltpu.VMEM(project_weight.shape, BF16),
            pltpu.VMEM((chain, pair, width), BF16),
            pltpu.VMEM((chain, 2, n_blk * pair, width), BF16),
            pltpu.VMEM((chain, heads, pair, 2 * HEAD_DIM), F32),
            pltpu.VMEM((chain, heads, pair, HEAD_DIM), F32),
            pltpu.VMEM((n_seq, rows // 2, 2 * noisy_latent.shape[1]), BF16),
            pltpu.VMEM((n_seq, rows // 2, 2 * noisy_latent.shape[1]), BF16),
            pltpu.VMEM((LATENT_CH, TILE_VOX), BF16),
            pltpu.VMEM((4, rows, TILE_VOX), BF16),
            dma((2,)),
            dma((chain, 3)),
            dma((chain, 2)),
            dma((chain, n_blk)),
            dma((chain, n_blk)),
            dma((n_seq,)),
            dma((n_seq,)),
            dma((chain * n_blk,)),
            dma((chain * n_blk,)),
            dma,
            dma,
        ],
        compiler_params=pltpu.CompilerParams(
            collective_id=0, has_side_effects=True, vmem_limit_bytes=56 * 2**20
        ),
        name="attention_to_tiles",
    )(tokens, project_weight, noisy_latent, final_weight)


REGION_ROWS = 4 * TILE_PH
REGION_COLS = 4 * TILE_PW
FRAME = REGION_ROWS * REGION_COLS
TAPS = 9 * LATENT_CH
BLOCK_CH = 128


def decode_kernel(
    n_blk,
    count_ref,
    inter_ref,
    tiles_ref,
    weight_ref,
    gain_ref,
    shift_ref,
    out_ref,
    weight_first,
    weight_second,
    gain_col,
    shift_col,
    place,
    patches,
):
    slot = pl.program_id(0)
    block = pl.program_id(1)
    rank = lax.axis_index("seq") * n_blk + lax.axis_index("blk")
    channels = weight_ref.shape[1]
    half_vox = TILE_VOX // TILE_F

    @pl.when((slot == 0) & (block == 0))
    def prepare():
        taps = [weight_ref[pl.ds(a * TAPS, TAPS), :].astype(F32) for a in range(3)]
        early = taps[0] + taps[1]
        weight_first[...] = (early + taps[2]).T.astype(BF16)
        weight_second[...] = jnp.concatenate([early, taps[2]], axis=0).T.astype(BF16)
        gain_col[...] = jnp.broadcast_to(gain_ref[...], (128, channels)).T
        shift_col[...] = jnp.broadcast_to(shift_ref[...], (128, channels)).T
        source = lax.broadcasted_iota(jnp.int32, (2 * half_vox, 2 * half_vox), 0)
        target = lax.broadcasted_iota(jnp.int32, (2 * half_vox, 2 * half_vox), 1)
        wanted = ((source >> 4) & 15) * REGION_COLS + (source >> 8) * 16 + (source & 15)
        place[...] = jnp.where(wanted == target, 1.0, 0.0).astype(BF16)

    own_count = count_ref[rank]
    filled = slot < own_count

    @pl.when(filled & (block == 0))
    def gather():
        first = lax.fori_loop(0, rank, lambda i, total: total + count_ref[i], 0)
        pixel = first + slot
        pieces = [tiles_ref[inter_ref[pixel * 4 + k]] for k in range(4)]
        stack = []
        for frame in range(TILE_F):
            lanes = slice(frame * half_vox, (frame + 1) * half_vox)
            for side in range(2):
                stack.append(
                    jnp.concatenate(
                        [pieces[2 * side][:, lanes], pieces[2 * side + 1][:, lanes]], axis=1
                    )
                )
        strips = jnp.dot(jnp.concatenate(stack, axis=0), place[...], preferred_element_type=F32)
        frames = []
        for frame in range(TILE_F):
            base = frame * 2 * LATENT_CH
            frames.append(
                jnp.concatenate(
                    [strips[base : base + LATENT_CH], strips[base + LATENT_CH : base + 2 * LATENT_CH]],
                    axis=1,
                )
            )
        region = jnp.concatenate(frames, axis=0)
        lane = lax.broadcasted_iota(jnp.int32, region.shape, 1)
        column = lane & (REGION_COLS - 1)
        row = lane >> 5
        by_row = [
            jnp.where(row == 0, region, pltpu.roll(region, REGION_COLS, 1)),
            region,
            jnp.where(row == REGION_ROWS - 1, region, pltpu.roll(region, FRAME - REGION_COLS, 1)),
        ]
        for b in range(3):
            moved = by_row[b]
            by_col = [
                jnp.where(column == 0, moved, pltpu.roll(moved, 1, 1)),
                moved,
                jnp.where(column == REGION_COLS - 1, moved, pltpu.roll(moved, FRAME - 1, 1)),
            ]
            for g in range(3):
                tap = by_col[g].astype(BF16)
                for frame in range(TILE_F):
                    patches[pl.ds(frame * TAPS + (b * 3 + g) * LATENT_CH, LATENT_CH), :] = tap[
                        frame * LATENT_CH : (frame + 1) * LATENT_CH
                    ]

    @pl.when(filled)
    def convolve():
        some = pl.ds(pl.multiple_of(block * BLOCK_CH, BLOCK_CH), BLOCK_CH)
        group = channels // GROUPS
        parts = [
            jnp.dot(weight_first[some, :], patches[:TAPS, :], preferred_element_type=F32),
            jnp.dot(weight_second[some, :], patches[...], preferred_element_type=F32),
        ]
        parts = [x.reshape(BLOCK_CH // group, group, FRAME) for x in parts]
        inv = 1.0 / (group * TILE_F * FRAME)
        mean = jnp.sum(parts[0] + parts[1], axis=(1, 2), keepdims=True) * inv
        spread = jnp.square(parts[0] - mean) + jnp.square(parts[1] - mean)
        var = jnp.sum(spread, axis=(1, 2), keepdims=True) * inv
        gain = gain_col[some, :][:, :1].reshape(BLOCK_CH // group, group, 1)
        shift = shift_col[some, :][:, :1].reshape(BLOCK_CH // group, group, 1)
        slope = 0.5 * gain * lax.rsqrt(var + norm_eps)
        offset = 0.5 * shift - mean * slope
        for frame in range(TILE_F):
            half = parts[frame] * slope + offset
            value = half + half * jnp.tanh(half)
            out_ref[0, 0, :, pl.ds(frame * FRAME, FRAME)] = value.reshape(BLOCK_CH, FRAME).astype(
                BF16
            )

    @pl.when(jnp.logical_not(filled))
    def clear():
        out_ref[...] = jnp.zeros(out_ref.shape, BF16)


def decode(n_blk, tiles, conv_weight, norm_gain, norm_shift, owner_count, intersection):
    channels = conv_weight.shape[1]
    voxels = TILE_F * FRAME
    whole = lambda *shape: pl.BlockSpec(shape, lambda i, j, *_: (0,) * len(shape))
    return pl.pallas_call(
        functools.partial(decode_kernel, n_blk),
        out_shape=jax.ShapeDtypeStruct((1, MAXPIX, channels, voxels), BF16),
        grid_spec=pltpu.PrefetchScalarGridSpec(
            num_scalar_prefetch=2,
            grid=(MAXPIX, channels // BLOCK_CH),
            in_specs=[
                whole(*tiles.shape),
                whole(*conv_weight.shape),
                whole(1, channels),
                whole(1, channels),
            ],
            out_specs=pl.BlockSpec((1, 1, BLOCK_CH, voxels), lambda i, j, *_: (0, i, j, 0)),
            scratch_shapes=[
                pltpu.VMEM((channels, TAPS), BF16),
                pltpu.VMEM((channels, 2 * TAPS), BF16),
                pltpu.VMEM((channels, 128), F32),
                pltpu.VMEM((channels, 128), F32),
                pltpu.VMEM((TILE_VOX, TILE_VOX), BF16),
                pltpu.VMEM((2 * TAPS, FRAME), BF16),
            ],
        ),
        compiler_params=pltpu.CompilerParams(vmem_limit_bytes=48 * 2**20),
        name="decode_tiles",
    )(
        owner_count,
        intersection.reshape(-1),
        tiles,
        conv_weight,
        norm_gain.reshape(1, -1),
        norm_shift.reshape(1, -1),
    )


def body(
    n_seq,
    n_blk,
    tokens,
    project_weight,
    noisy_latent,
    final_weight,
    conv_weight,
    norm_gain,
    norm_shift,
    owner_count,
    intersection,
):
    tiles = latent_tiles(n_seq, n_blk, tokens, project_weight, noisy_latent, final_weight)
    tiles = tiles.reshape(-1, LATENT_CH, TILE_VOX)
    return decode(n_blk, tiles, conv_weight, norm_gain, norm_shift, owner_count, intersection)


def solution(mesh):
    return jax.shard_map(
        functools.partial(body, mesh.shape["seq"], mesh.shape["blk"]),
        mesh=mesh,
        in_specs=(
            P(("seq", "blk"), None),
            P(None, None, "seq"),
            P(("seq", "blk"), None),
            P(),
            P(),
            P(),
            P(),
            P(),
            P(),
        ),
        out_specs=P(("seq", "blk"), None, None, None),
        check_vma=False,
    )
```

```python
import functools
import math

import jax
import jax.numpy as jnp
from jax import lax
from jax.experimental import pallas as pl
from jax.experimental.pallas import tpu as pltpu
from jax.sharding import PartitionSpec as P

HEAD_DIM = 128
LATENT_CH = 16
GROUPS = 32
TILE_F = 2
TILE_PH = 8
TILE_PW = 8
MAXPIX = 4

scale_factor = 0.476986
step_size = 0.25
norm_eps = 1e-06

REGION_ROWS = 4 * TILE_PH
REGION_COLS = 4 * TILE_PW
FRAME = REGION_ROWS * REGION_COLS
TAPS = 9 * LATENT_CH
BLOCK_CH = 256
SUB_CH = 128
MESH = pl.DeviceIdType.MESH
F32 = jnp.float32
BF16 = jnp.bfloat16
TILE_VOX = TILE_F * 4 * TILE_PH * TILE_PW


def nt_dot(a, b):
    return lax.dot_general(a, b, (((1,), (1,)), ((), ())), preferred_element_type=F32)


def attention_kernel(
    chain,
    n_blk,
    tokens_ref,
    weight_ref,
    noisy_ref,
    final_ref,
    conv_ref,
    gain_ref,
    shift_ref,
    tiles_ref,
    first_ref,
    second_ref,
    affine_ref,
    place_ref,
    tok,
    weight,
    q_all,
    kv_all,
    acc_all,
    max_all,
    vel_out,
    vel_in,
    own_tile,
    spread,
    first,
    second,
    affine,
    place,
    local_sem,
    keep_sem,
    tok_send,
    tok_recv,
    kv_send,
    kv_recv,
    vel_send,
    vel_recv,
    tile_send,
    tile_recv,
    sib_send,
    sib_recv,
):
    n_seq = 2 * chain
    seq = lax.axis_index("seq")
    blk = lax.axis_index("blk")
    z = lax.div(seq, 2)
    core = lax.rem(seq, 2)
    me = seq * n_blk + blk
    rows = tokens_ref.shape[0]
    half = rows // 2
    width = q_all.shape[2]
    heads = width // HEAD_DIM

    load_weight = pltpu.make_async_copy(weight_ref, weight, local_sem.at[0])
    load_weight.start()
    load_tokens = []
    for part in range(2):
        load_tokens.append(
            pltpu.make_async_copy(
                tokens_ref.at[pl.ds(part * half, half)],
                tok.at[z, part, core],
                local_sem.at[1 + part],
            )
        )
        load_tokens[part].start()

    barrier = pltpu.get_barrier_semaphore()

    def greet(step, carry):
        other = lax.rem(me + step, n_seq * n_blk)
        pl.semaphore_signal(
            barrier,
            inc=1,
            device_id=(lax.div(other, n_blk), lax.rem(other, n_blk)),
            device_id_type=MESH,
        )
        return carry

    lax.fori_loop(1, n_seq * n_blk, greet, 0)
    pl.semaphore_wait(barrier, n_seq * n_blk - 1)

    def tok_copy(origin, part, side, target_z, target_core):
        if origin is None:
            origin, source = z, tokens_ref.at[pl.ds(part * half, half)]
        else:
            source = tok.at[origin, part, core]
        return pltpu.make_async_remote_copy(
            src_ref=source,
            dst_ref=tok.at[origin, part, core],
            send_sem=tok_send.at[origin, part, side],
            recv_sem=tok_recv.at[origin, part, core],
            device_id=(target_z * 2 + target_core, blk),
            device_id_type=MESH,
        )

    def tok_arrival(origin, part, origin_core):
        pltpu.make_async_remote_copy(
            src_ref=tok.at[origin, part, origin_core],
            dst_ref=tok.at[origin, part, origin_core],
            send_sem=tok_send.at[origin, part, 0],
            recv_sem=tok_recv.at[origin, part, origin_core],
            device_id=(z * 2 + 1 - core, blk),
            device_id_type=MESH,
        ).wait_recv()

    def go_left(origin, part):
        return tok_copy(origin, part, 0, z - 1, core)

    def go_right(origin, part):
        return tok_copy(origin, part, 1, z + 1, core)

    def go_over(origin, part):
        return tok_copy(origin, part, 2, z, 1 - core)

    def kv_place(origin, part, source):
        return kv_all.at[origin, part, :, pl.ds(pl.multiple_of(source * rows, rows), rows), :]

    def kv_copy(origin, part, hop):
        return pltpu.make_async_remote_copy(
            src_ref=kv_place(origin, part, blk),
            dst_ref=kv_place(origin, part, blk),
            send_sem=kv_send.at[origin, part, hop],
            recv_sem=kv_recv.at[origin, part, blk],
            device_id=(seq, lax.rem(blk + hop, n_blk)),
            device_id_type=MESH,
        )

    def kv_arrival(origin, part, hop):
        source = lax.rem(blk + n_blk - hop, n_blk)
        pltpu.make_async_remote_copy(
            src_ref=kv_place(origin, part, source),
            dst_ref=kv_place(origin, part, source),
            send_sem=kv_send.at[origin, part, hop],
            recv_sem=kv_recv.at[origin, part, source],
            device_id=(seq, lax.rem(blk + hop, n_blk)),
            device_id_type=MESH,
        ).wait_recv()

    def project(origin, part):
        x = tok[origin, part].reshape(rows, tok.shape[4])
        own = pl.ds(pl.multiple_of(blk * rows, rows), rows)
        for kind in range(2):
            kv_all[origin, part, kind, own, :] = jnp.dot(
                x, weight[kind + 1], preferred_element_type=F32
            ).astype(BF16)
        for hop in range(1, n_blk):
            kv_copy(origin, part, hop).start()
        query = jnp.dot(x, weight[0], preferred_element_type=F32)
        query = (query * (HEAD_DIM**-0.5 * math.log2(math.e))).astype(BF16)
        some = pl.ds(part * rows, rows)
        q_all[origin, some, :] = query
        for head in range(heads):
            max_all[origin, head, some, :] = jnp.full((rows, HEAD_DIM), -1e30, F32)
            acc_all[origin, head, some, :] = jnp.zeros((rows, 2 * HEAD_DIM), F32)

    def attend(q_pair, kv_pair, part):
        for head in range(heads):
            lanes = pl.ds(head * HEAD_DIM, HEAD_DIM)
            scores = nt_dot(q_all[q_pair, :, lanes], kv_all[kv_pair, part, 0, :, lanes])
            old_max = max_all[q_pair, head]
            new_max = jnp.maximum(old_max, jnp.max(scores, axis=1, keepdims=True))
            rescale = jnp.exp2(old_max - new_max)
            weights = jnp.exp2(scores - new_max[:, :1]).astype(BF16)
            value = kv_all[kv_pair, part, 1, :, lanes]
            value = jnp.concatenate([value, jnp.ones_like(value)], axis=1)
            product = jnp.dot(weights, value, preferred_element_type=F32)
            acc_all[q_pair, head] = (
                acc_all[q_pair, head] * jnp.concatenate([rescale, rescale], axis=1) + product
            )
            max_all[q_pair, head] = new_max

    def each_of_step(step, action):
        if step >= chain:
            return
        if step == 0:
            action(z, None)
            return
        pl.when(z - step >= 0)(lambda: action(z - step, "left"))
        pl.when(z + step < chain)(lambda: action(z + step, "right"))

    def over_known(radius, action):
        low = jnp.maximum(z - radius, 0)
        high = jnp.minimum(z + radius, chain - 1) + 1

        def one(index, carry):
            action(index)
            return carry

        lax.fori_loop(low, high, one, 0)

    def forward(part):
        def action(origin, side):
            tok_arrival(origin, part, core)
            if side == "left":
                pl.when(z < chain - 1)(lambda: go_right(origin, part).start())
            else:
                pl.when(z > 0)(lambda: go_left(origin, part).start())
            go_over(origin, part).start()

        return action

    def project_arrived(part):
        def action(origin, side):
            tok_arrival(origin, part, 1 - core)
            project(origin, part)

        return action

    for part in range(2):
        pl.when(z > 0)(lambda: go_left(None, part).start())
        pl.when(z < chain - 1)(lambda: go_right(None, part).start())
        go_over(None, part).start()

    def prepare():
        token = lax.broadcasted_iota(jnp.int32, (rows, TILE_VOX), 0)
        voxel = lax.broadcasted_iota(jnp.int32, (rows, TILE_VOX), 1)
        row, column = (voxel >> 4) & 15, voxel & 15
        home = (voxel >> 8) * (TILE_PH * TILE_PW) + (row >> 1) * TILE_PW + (column >> 1)
        for sub in range(4):
            hit = (home == token) & ((row & 1) * 2 + (column & 1) == sub)
            spread[sub] = jnp.where(hit, 1.0, 0.0).astype(BF16)
        taps = [conv_ref[pl.ds(a * TAPS, TAPS), :].astype(F32) for a in range(3)]
        early = taps[0] + taps[1]
        first[...] = (early + taps[2]).T.astype(BF16)
        second[...] = jnp.concatenate([early, taps[2]], axis=0).T.astype(BF16)
        channels = conv_ref.shape[1]
        index = lax.broadcasted_iota(jnp.int32, (128, channels), 0)
        affine[...] = jnp.where(index == 0, gain_ref[...], shift_ref[...]).T
        source = lax.broadcasted_iota(jnp.int32, place.shape, 0)
        target = lax.broadcasted_iota(jnp.int32, place.shape, 1)
        wanted = ((source >> 4) & 15) * REGION_COLS + (source >> 8) * 16 + (source & 15)
        place[...] = jnp.where(wanted == target, 1.0, 0.0).astype(BF16)
        for copy in keeps:
            copy.start()

    keeps = [
        pltpu.make_async_copy(source, target, keep_sem.at[number])
        for number, (source, target) in enumerate(
            [(first, first_ref), (second, second_ref), (affine, affine_ref), (place, place_ref)]
        )
    ]

    load_weight.wait()
    load_tokens[0].wait()
    load_tokens[1].wait()
    for part in range(2):
        project_arrived(part)(z, None)

    def attend_both(q_pair, kv_pair):
        attend(q_pair, kv_pair, 0)
        attend(q_pair, kv_pair, 1)

    for turn in range(2 * chain):
        step, part = turn // 2, turn % 2
        if turn >= 1:
            each_of_step((turn + 1) // 2, forward((turn + 1) % 2))
            each_of_step((turn + 1) // 2, project_arrived((turn + 1) % 2))
        if turn == 0:
            prepare()
        if part == 0 and step >= 1:
            each_of_step(
                step, lambda o, side: over_known(step - 1, lambda other: attend_both(o, other))
            )

        def meet(origin, side):
            for hop in range(1, n_blk):
                kv_arrival(origin, part, hop)
            over_known(step, lambda other: attend(other, origin, part))

        each_of_step(step, meet)

    final = final_ref[:, pl.ds(pl.multiple_of(seq * width, width), width)]

    def vel_copy(target_z, target_core):
        target = target_z * 2 + target_core
        return pltpu.make_async_remote_copy(
            src_ref=vel_out.at[target],
            dst_ref=vel_in.at[seq],
            send_sem=vel_send.at[target],
            recv_sem=vel_recv.at[seq],
            device_id=(target, blk),
            device_id_type=MESH,
        )

    for turn in range(chain):
        q_pair = lax.rem(z + 1 + turn, chain)
        attended = []
        for head in range(heads):
            total = acc_all[q_pair, head]
            attended.append((total[:, :HEAD_DIM] / total[:, HEAD_DIM:]).astype(BF16))
        attended = jnp.concatenate(attended, axis=1)
        for side in range(2):
            own = [
                attended[part * rows + side * half : part * rows + (side + 1) * half]
                for part in range(2)
            ]
            vel_out[q_pair * 2 + side] = nt_dot(final, jnp.concatenate(own, axis=0)).astype(BF16)
        if turn < chain - 1:
            for side in range(2):
                vel_copy(q_pair, side).start()
        else:
            vel_copy(z, 1 - core).start()
    vel_in[seq] = vel_out[seq]

    def vel_arrival(hop, carry):
        source = lax.rem(seq + hop, n_seq)
        pltpu.make_async_remote_copy(
            src_ref=vel_out.at[source],
            dst_ref=vel_in.at[source],
            send_sem=vel_send.at[source],
            recv_sem=vel_recv.at[source],
            device_id=(source, blk),
            device_id_type=MESH,
        ).wait_recv()
        return carry

    lax.fori_loop(1, n_seq, vel_arrival, 0)
    velocity = vel_in[0].astype(F32)
    for source in range(1, n_seq):
        velocity = velocity + vel_in[source].astype(F32)
    patch = noisy_ref.shape[0]
    latent = ((noisy_ref[...] - step_size * velocity) / scale_factor).astype(BF16)
    channel = lax.broadcasted_iota(jnp.int32, (LATENT_CH, patch), 0)
    feature = lax.broadcasted_iota(jnp.int32, (LATENT_CH, patch), 1)
    tile = jnp.zeros((LATENT_CH, TILE_VOX), F32)
    for sub in range(4):
        pick = jnp.where(feature == channel * 4 + sub, 1.0, 0.0).astype(BF16)
        tile = tile + jnp.dot(
            jnp.dot(pick, latent, preferred_element_type=F32).astype(BF16),
            spread[sub],
            preferred_element_type=F32,
        )
    own_tile[...] = tile.astype(BF16)

    n_same = chain * n_blk
    index = z * n_blk + blk
    keep = pltpu.make_async_copy(own_tile, tiles_ref.at[z, core, blk], local_sem.at[0])
    keep.start()

    def tile_copy(hop):
        other = lax.rem(index + hop, n_same)
        return pltpu.make_async_remote_copy(
            src_ref=own_tile,
            dst_ref=tiles_ref.at[z, core, blk],
            send_sem=tile_send.at[hop],
            recv_sem=tile_recv.at[index],
            device_id=(lax.div(other, n_blk) * 2 + core, lax.rem(other, n_blk)),
            device_id_type=MESH,
        )

    def tile_start(hop, carry):
        tile_copy(hop).start()
        return carry

    def tile_arrival(hop, carry):
        source = lax.rem(index + n_same - hop, n_same)
        pltpu.make_async_remote_copy(
            src_ref=own_tile,
            dst_ref=tiles_ref.at[lax.div(source, n_blk), core, lax.rem(source, n_blk)],
            send_sem=tile_send.at[hop],
            recv_sem=tile_recv.at[source],
            device_id=(lax.div(source, n_blk) * 2 + core, lax.rem(source, n_blk)),
            device_id_type=MESH,
        ).wait_recv()
        return carry

    lax.fori_loop(1, n_same, tile_start, 0)
    keep.wait()
    lax.fori_loop(1, n_same, tile_arrival, 0)
    over = pltpu.make_async_remote_copy(
        src_ref=tiles_ref.at[:, core],
        dst_ref=tiles_ref.at[:, core],
        send_sem=sib_send,
        recv_sem=sib_recv,
        device_id=(z * 2 + 1 - core, blk),
        device_id_type=MESH,
    )
    over.start()

    for part in range(2):
        pl.when(z > 0)(lambda: go_left(None, part).wait_send())
        pl.when(z < chain - 1)(lambda: go_right(None, part).wait_send())
        go_over(None, part).wait_send()

        def settle(origin, side):
            if side == "left":
                pl.when(z < chain - 1)(lambda: go_right(origin, part).wait_send())
            else:
                pl.when(z > 0)(lambda: go_left(origin, part).wait_send())
            go_over(origin, part).wait_send()

        for step in range(1, chain):
            each_of_step(step, settle)

    def settle_kv(origin, carry):
        for part in range(2):
            for hop in range(1, n_blk):
                kv_copy(origin, part, hop).wait_send()
        return carry

    lax.fori_loop(0, chain, settle_kv, 0)
    for copy in keeps:
        copy.wait()

    def settle_vel(hop, carry):
        other = lax.rem(seq + hop, n_seq)
        vel_copy(lax.div(other, 2), lax.rem(other, 2)).wait_send()
        return carry

    lax.fori_loop(1, n_seq, settle_vel, 0)

    def settle_tile(hop, carry):
        tile_copy(hop).wait_send()
        return carry

    lax.fori_loop(1, n_same, settle_tile, 0)
    over.wait_send()
    pltpu.make_async_remote_copy(
        src_ref=tiles_ref.at[:, 1 - core],
        dst_ref=tiles_ref.at[:, 1 - core],
        send_sem=sib_send,
        recv_sem=sib_recv,
        device_id=(z * 2 + 1 - core, blk),
        device_id_type=MESH,
    ).wait_recv()


def latent_tiles(
    n_seq, n_blk, tokens, project_weight, noisy_latent, final_weight, conv_weight, gain, shift
):
    chain = n_seq // 2
    rows, depth = tokens.shape
    width = project_weight.shape[2]
    channels = conv_weight.shape[1]
    heads = width // HEAD_DIM
    pair = 2 * rows
    dma = pltpu.SemaphoreType.DMA
    vmem = pl.BlockSpec(memory_space=pltpu.VMEM)
    hbm = pl.BlockSpec(memory_space=pl.ANY)
    kept = [
        ((channels, TAPS), BF16),
        ((channels, 2 * TAPS), BF16),
        ((channels, 128), F32),
        ((TILE_VOX, TILE_VOX), BF16),
    ]
    return pl.pallas_call(
        functools.partial(attention_kernel, chain, n_blk),
        out_shape=[jax.ShapeDtypeStruct((chain, 2, n_blk, LATENT_CH, TILE_VOX), BF16)]
        + [jax.ShapeDtypeStruct(*one) for one in kept],
        in_specs=[hbm, hbm] + [vmem] * 5,
        out_specs=[hbm] * 5,
        scratch_shapes=[
            pltpu.VMEM((chain, 2, 2, rows // 2, depth), BF16),
            pltpu.VMEM(project_weight.shape, BF16),
            pltpu.VMEM((chain, pair, width), BF16),
            pltpu.VMEM((chain, 2, 2, n_blk * rows, width), BF16),
            pltpu.VMEM((chain, heads, pair, 2 * HEAD_DIM), F32),
            pltpu.VMEM((chain, heads, pair, HEAD_DIM), F32),
            pltpu.VMEM((n_seq, noisy_latent.shape[0], rows), BF16),
            pltpu.VMEM((n_seq, noisy_latent.shape[0], rows), BF16),
            pltpu.VMEM((LATENT_CH, TILE_VOX), BF16),
            pltpu.VMEM((4, rows, TILE_VOX), BF16),
        ]
        + [pltpu.VMEM(*one) for one in kept]
        + [
            dma((3,)),
            dma((4,)),
            dma((chain, 2, 3)),
            dma((chain, 2, 2)),
            dma((chain, 2, n_blk)),
            dma((chain, 2, n_blk)),
            dma((n_seq,)),
            dma((n_seq,)),
            dma((chain * n_blk,)),
            dma((chain * n_blk,)),
            dma,
            dma,
        ],
        compiler_params=pltpu.CompilerParams(
            collective_id=0, has_side_effects=True, vmem_limit_bytes=60 * 2**20
        ),
        name="attention_to_tiles",
    )(tokens, project_weight, noisy_latent, final_weight, conv_weight, gain, shift)


def decode_kernel(
    n_blk,
    count_ref,
    inter_ref,
    tiles_ref,
    weight_first,
    weight_second,
    affine,
    place,
    out_ref,
    patches,
):
    slot = pl.program_id(0)
    block = pl.program_id(1)
    rank = lax.axis_index("seq") * n_blk + lax.axis_index("blk")
    channels = weight_first.shape[0]
    half_vox = TILE_VOX // TILE_F

    own_count = count_ref[rank]
    filled = slot < own_count

    @pl.when(filled & (block == 0))
    def gather():
        first = lax.fori_loop(0, rank, lambda i, total: total + count_ref[i], 0)
        pixel = first + slot
        pieces = [tiles_ref[inter_ref[k, pixel]] for k in range(4)]
        stack = []
        for frame in range(TILE_F):
            lanes = slice(frame * half_vox, (frame + 1) * half_vox)
            for side in range(2):
                stack.append(
                    jnp.concatenate(
                        [pieces[2 * side][:, lanes], pieces[2 * side + 1][:, lanes]], axis=1
                    )
                )
        strips = jnp.dot(jnp.concatenate(stack, axis=0), place[...], preferred_element_type=F32)
        frames = []
        for frame in range(TILE_F):
            base = frame * 2 * LATENT_CH
            frames.append(
                jnp.concatenate(
                    [strips[base : base + LATENT_CH], strips[base + LATENT_CH : base + 2 * LATENT_CH]],
                    axis=1,
                )
            )
        region = jnp.concatenate(frames, axis=0)
        lane = lax.broadcasted_iota(jnp.int32, region.shape, 1)
        column = lane & (REGION_COLS - 1)
        row = lane >> 5
        by_row = [
            jnp.where(row == 0, region, pltpu.roll(region, REGION_COLS, 1)),
            region,
            jnp.where(row == REGION_ROWS - 1, region, pltpu.roll(region, FRAME - REGION_COLS, 1)),
        ]
        for b in range(3):
            moved = by_row[b]
            by_col = [
                jnp.where(column == 0, moved, pltpu.roll(moved, 1, 1)),
                moved,
                jnp.where(column == REGION_COLS - 1, moved, pltpu.roll(moved, FRAME - 1, 1)),
            ]
            for g in range(3):
                tap = by_col[g].astype(BF16)
                for frame in range(TILE_F):
                    patches[pl.ds(frame * TAPS + (b * 3 + g) * LATENT_CH, LATENT_CH), :] = tap[
                        frame * LATENT_CH : (frame + 1) * LATENT_CH
                    ]

    group = channels // GROUPS
    inv = 1.0 / (group * TILE_F * FRAME)

    @pl.when(filled)
    def convolve():
        for sub in range(BLOCK_CH // SUB_CH):
            base = pl.multiple_of(block * BLOCK_CH + sub * SUB_CH, SUB_CH)
            some = pl.ds(base, SUB_CH)
            parts = [
                jnp.dot(weight_first[some, :], patches[:TAPS, :], preferred_element_type=F32),
                jnp.dot(weight_second[some, :], patches[...], preferred_element_type=F32),
            ]
            parts = [x.reshape(SUB_CH // group, group, FRAME) for x in parts]
            mean = jnp.sum(parts[0] + parts[1], axis=(1, 2), keepdims=True) * inv
            spread = jnp.square(parts[0] - mean) + jnp.square(parts[1] - mean)
            var = jnp.sum(spread, axis=(1, 2), keepdims=True) * inv
            both = affine[some, :]
            gain = both[:, 0:1].reshape(SUB_CH // group, group, 1)
            shift = both[:, 1:2].reshape(SUB_CH // group, group, 1)
            slope = 0.5 * gain * lax.rsqrt(var + norm_eps)
            offset = 0.5 * shift - mean * slope
            for frame in range(TILE_F):
                half = parts[frame] * slope + offset
                value = half + half * jnp.tanh(half)
                out_ref[0, 0, pl.ds(sub * SUB_CH, SUB_CH), pl.ds(frame * FRAME, FRAME)] = (
                    value.reshape(SUB_CH, FRAME).astype(BF16)
                )

    @pl.when(jnp.logical_not(filled))
    def clear():
        out_ref[...] = jnp.zeros(out_ref.shape, BF16)


def decode(n_blk, tiles, prepared, owner_count, intersection):
    channels = prepared[0].shape[0]
    voxels = TILE_F * FRAME
    whole = lambda x: pl.BlockSpec(x.shape, lambda i, j, *_: (0,) * x.ndim)
    return pl.pallas_call(
        functools.partial(decode_kernel, n_blk),
        out_shape=jax.ShapeDtypeStruct((1, MAXPIX, channels, voxels), BF16),
        grid_spec=pltpu.PrefetchScalarGridSpec(
            num_scalar_prefetch=2,
            grid=(MAXPIX, channels // BLOCK_CH),
            in_specs=[whole(tiles)] + [whole(x) for x in prepared],
            out_specs=pl.BlockSpec((1, 1, BLOCK_CH, voxels), lambda i, j, *_: (0, i, j, 0)),
            scratch_shapes=[pltpu.VMEM((2 * TAPS, FRAME), BF16)],
        ),
        compiler_params=pltpu.CompilerParams(vmem_limit_bytes=60 * 2**20),
        name="decode_tiles",
    )(owner_count, intersection.T, tiles, *prepared)


def body(
    n_seq,
    n_blk,
    tokens,
    project_weight,
    noisy_latent,
    final_weight,
    conv_weight,
    norm_gain,
    norm_shift,
    owner_count,
    intersection,
):
    tiles, *prepared = latent_tiles(
        n_seq,
        n_blk,
        tokens,
        project_weight,
        noisy_latent.T,
        final_weight.T,
        conv_weight,
        norm_gain.reshape(1, -1),
        norm_shift.reshape(1, -1),
    )
    tiles = tiles.reshape(-1, LATENT_CH, TILE_VOX)
    return decode(n_blk, tiles, prepared, owner_count, intersection)


def solution(mesh):
    return jax.shard_map(
        functools.partial(body, mesh.shape["seq"], mesh.shape["blk"]),
        mesh=mesh,
        in_specs=(
            P(("seq", "blk"), None),
            P(None, None, "seq"),
            P(("seq", "blk"), None),
            P(),
            P(),
            P(),
            P(),
            P(),
            P(),
        ),
        out_specs=P(("seq", "blk"), None, None, None),
        check_vma=False,
    )
```

```python
import functools
import math

import jax
import jax.numpy as jnp
from jax import lax
from jax.experimental import pallas as pl
from jax.experimental.pallas import tpu as pltpu
from jax.sharding import PartitionSpec as P

HEAD_DIM = 128
LATENT_CH = 16
GROUPS = 32
TILE_F = 2
TILE_PH = 8
TILE_PW = 8
MAXPIX = 4

scale_factor = 0.476986
step_size = 0.25
norm_eps = 1e-06

REGION_ROWS = 4 * TILE_PH
REGION_COLS = 4 * TILE_PW
FRAME = REGION_ROWS * REGION_COLS
TAPS = 9 * LATENT_CH
MESH = pl.DeviceIdType.MESH
F32 = jnp.float32
BF16 = jnp.bfloat16
TILE_VOX = TILE_F * 4 * TILE_PH * TILE_PW


def nt_dot(a, b):
    return lax.dot_general(a, b, (((1,), (1,)), ((), ())), preferred_element_type=F32)


def attention_kernel(
    chain,
    n_blk,
    tokens_ref,
    weight_ref,
    noisy_ref,
    final_ref,
    conv_ref,
    gain_ref,
    shift_ref,
    tiles_ref,
    first_ref,
    second_ref,
    affine_ref,
    place_ref,
    tok,
    weight,
    q_all,
    kv_all,
    acc_all,
    max_all,
    vel_out,
    vel_in,
    own_tile,
    spread,
    first,
    second,
    affine,
    place,
    local_sem,
    keep_sem,
    tok_send,
    tok_recv,
    kv_send,
    kv_recv,
    vel_send,
    vel_recv,
    tile_send,
    tile_recv,
    over_send,
    over_recv,
):
    n_seq = 2 * chain
    seq = lax.axis_index("seq")
    blk = lax.axis_index("blk")
    z = lax.div(seq, 2)
    core = lax.rem(seq, 2)
    me = seq * n_blk + blk
    rows = tokens_ref.shape[0]
    half = rows // 2
    width = q_all.shape[2]
    heads = width // HEAD_DIM

    load_weight = pltpu.make_async_copy(weight_ref, weight, local_sem.at[0])
    load_weight.start()
    load_tokens = []
    for part in range(2):
        load_tokens.append(
            pltpu.make_async_copy(
                tokens_ref.at[pl.ds(part * half, half)],
                tok.at[z, part, core],
                local_sem.at[1 + part],
            )
        )
        load_tokens[part].start()

    barrier = pltpu.get_barrier_semaphore()

    def greet(step, carry):
        other = lax.rem(me + step, n_seq * n_blk)
        pl.semaphore_signal(
            barrier,
            inc=1,
            device_id=(lax.div(other, n_blk), lax.rem(other, n_blk)),
            device_id_type=MESH,
        )
        return carry

    lax.fori_loop(1, n_seq * n_blk, greet, 0)
    pl.semaphore_wait(barrier, n_seq * n_blk - 1)

    def tok_copy(origin, part, side, target_z, target_core):
        if origin is None:
            origin, source = z, tokens_ref.at[pl.ds(part * half, half)]
        else:
            source = tok.at[origin, part, core]
        return pltpu.make_async_remote_copy(
            src_ref=source,
            dst_ref=tok.at[origin, part, core],
            send_sem=tok_send.at[origin, part, side],
            recv_sem=tok_recv.at[origin, part, core],
            device_id=(target_z * 2 + target_core, blk),
            device_id_type=MESH,
        )

    def tok_arrival(origin, part, origin_core):
        pltpu.make_async_remote_copy(
            src_ref=tok.at[origin, part, origin_core],
            dst_ref=tok.at[origin, part, origin_core],
            send_sem=tok_send.at[origin, part, 0],
            recv_sem=tok_recv.at[origin, part, origin_core],
            device_id=(z * 2 + 1 - core, blk),
            device_id_type=MESH,
        ).wait_recv()

    def go_left(origin, part):
        return tok_copy(origin, part, 0, z - 1, core)

    def go_right(origin, part):
        return tok_copy(origin, part, 1, z + 1, core)

    def go_over(origin, part):
        return tok_copy(origin, part, 2, z, 1 - core)

    def kv_place(origin, part, source):
        return kv_all.at[origin, part, :, pl.ds(pl.multiple_of(source * rows, rows), rows), :]

    def kv_copy(origin, part, hop):
        return pltpu.make_async_remote_copy(
            src_ref=kv_place(origin, part, blk),
            dst_ref=kv_place(origin, part, blk),
            send_sem=kv_send.at[origin, part, hop],
            recv_sem=kv_recv.at[origin, part, blk],
            device_id=(seq, lax.rem(blk + hop, n_blk)),
            device_id_type=MESH,
        )

    def kv_arrival(origin, part, hop):
        source = lax.rem(blk + n_blk - hop, n_blk)
        pltpu.make_async_remote_copy(
            src_ref=kv_place(origin, part, source),
            dst_ref=kv_place(origin, part, source),
            send_sem=kv_send.at[origin, part, hop],
            recv_sem=kv_recv.at[origin, part, source],
            device_id=(seq, lax.rem(blk + hop, n_blk)),
            device_id_type=MESH,
        ).wait_recv()

    def project(origin, part):
        x = tok[origin, part].reshape(rows, tok.shape[4])
        own = pl.ds(pl.multiple_of(blk * rows, rows), rows)
        for kind in range(2):
            kv_all[origin, part, kind, own, :] = jnp.dot(
                x, weight[kind + 1], preferred_element_type=F32
            ).astype(BF16)
        for hop in range(1, n_blk):
            kv_copy(origin, part, hop).start()
        query = jnp.dot(x, weight[0], preferred_element_type=F32)
        query = (query * (HEAD_DIM**-0.5 * math.log2(math.e))).astype(BF16)
        some = pl.ds(part * rows, rows)
        q_all[origin, some, :] = query
        for head in range(heads):
            max_all[origin, head, some, :] = jnp.full((rows, HEAD_DIM), -1e30, F32)
            acc_all[origin, head, some, :] = jnp.zeros((rows, 2 * HEAD_DIM), F32)

    def attend(q_pair, kv_pair, part):
        for head in range(heads):
            lanes = pl.ds(head * HEAD_DIM, HEAD_DIM)
            scores = nt_dot(q_all[q_pair, :, lanes], kv_all[kv_pair, part, 0, :, lanes])
            old_max = max_all[q_pair, head]
            new_max = jnp.maximum(old_max, jnp.max(scores, axis=1, keepdims=True))
            rescale = jnp.exp2(old_max - new_max)
            weights = jnp.exp2(scores - new_max[:, :1]).astype(BF16)
            value = kv_all[kv_pair, part, 1, :, lanes]
            value = jnp.concatenate([value, jnp.ones_like(value)], axis=1)
            product = jnp.dot(weights, value, preferred_element_type=F32)
            acc_all[q_pair, head] = (
                acc_all[q_pair, head] * jnp.concatenate([rescale, rescale], axis=1) + product
            )
            max_all[q_pair, head] = new_max

    def each_of_step(step, action):
        if step >= chain:
            return
        if step == 0:
            action(z, None)
            return
        pl.when(z - step >= 0)(lambda: action(z - step, "left"))
        pl.when(z + step < chain)(lambda: action(z + step, "right"))

    def over_known(radius, action):
        low = jnp.maximum(z - radius, 0)
        high = jnp.minimum(z + radius, chain - 1) + 1

        def one(index, carry):
            action(index)
            return carry

        lax.fori_loop(low, high, one, 0)

    def forward(part):
        def action(origin, side):
            tok_arrival(origin, part, core)
            if side == "left":
                pl.when(z < chain - 1)(lambda: go_right(origin, part).start())
            else:
                pl.when(z > 0)(lambda: go_left(origin, part).start())
            go_over(origin, part).start()

        return action

    def project_arrived(part):
        def action(origin, side):
            tok_arrival(origin, part, 1 - core)
            project(origin, part)

        return action

    for part in range(2):
        pl.when(z > 0)(lambda: go_left(None, part).start())
        pl.when(z < chain - 1)(lambda: go_right(None, part).start())
        go_over(None, part).start()

    def prepare():
        token = lax.broadcasted_iota(jnp.int32, (rows, TILE_VOX), 0)
        voxel = lax.broadcasted_iota(jnp.int32, (rows, TILE_VOX), 1)
        row, column = (voxel >> 4) & 15, voxel & 15
        home = (voxel >> 8) * (TILE_PH * TILE_PW) + (row >> 1) * TILE_PW + (column >> 1)
        for sub in range(4):
            hit = (home == token) & ((row & 1) * 2 + (column & 1) == sub)
            spread[sub] = jnp.where(hit, 1.0, 0.0).astype(BF16)
        taps = [conv_ref[pl.ds(a * TAPS, TAPS), :].astype(F32) for a in range(3)]
        early = taps[0] + taps[1]
        first[...] = (early + taps[2]).T.astype(BF16)
        second[...] = jnp.concatenate([early, taps[2]], axis=0).T.astype(BF16)
        channels = conv_ref.shape[1]
        index = lax.broadcasted_iota(jnp.int32, (128, channels), 0)
        affine[...] = jnp.where(index == 0, gain_ref[...], shift_ref[...]).T
        source = lax.broadcasted_iota(jnp.int32, place.shape, 0)
        target = lax.broadcasted_iota(jnp.int32, place.shape, 1)
        wanted = ((source >> 4) & 15) * REGION_COLS + (source >> 8) * 16 + (source & 15)
        place[...] = jnp.where(wanted == target, 1.0, 0.0).astype(BF16)
        for copy in keeps:
            copy.start()

    keeps = [
        pltpu.make_async_copy(source, target, keep_sem.at[number])
        for number, (source, target) in enumerate(
            [(first, first_ref), (second, second_ref), (affine, affine_ref), (place, place_ref)]
        )
    ]

    load_weight.wait()
    load_tokens[0].wait()
    load_tokens[1].wait()
    for part in range(2):
        project_arrived(part)(z, None)

    def attend_both(q_pair, kv_pair):
        attend(q_pair, kv_pair, 0)
        attend(q_pair, kv_pair, 1)

    for turn in range(2 * chain):
        step, part = turn // 2, turn % 2
        if turn >= 1:
            each_of_step((turn + 1) // 2, forward((turn + 1) % 2))
            each_of_step((turn + 1) // 2, project_arrived((turn + 1) % 2))
        if turn == 0:
            prepare()
        if part == 0 and step >= 1:
            each_of_step(
                step, lambda o, side: over_known(step - 1, lambda other: attend_both(o, other))
            )

        def meet(origin, side):
            for hop in range(1, n_blk):
                kv_arrival(origin, part, hop)
            over_known(step, lambda other: attend(other, origin, part))

        each_of_step(step, meet)

    final = final_ref[:, pl.ds(pl.multiple_of(seq * width, width), width)]

    def vel_copy(target_z, target_core):
        target = target_z * 2 + target_core
        return pltpu.make_async_remote_copy(
            src_ref=vel_out.at[target],
            dst_ref=vel_in.at[seq],
            send_sem=vel_send.at[target],
            recv_sem=vel_recv.at[seq],
            device_id=(target, blk),
            device_id_type=MESH,
        )

    for turn in range(chain):
        q_pair = lax.rem(z + 1 + turn, chain)
        attended = []
        for head in range(heads):
            total = acc_all[q_pair, head]
            attended.append((total[:, :HEAD_DIM] / total[:, HEAD_DIM:]).astype(BF16))
        attended = jnp.concatenate(attended, axis=1)
        for side in range(2):
            own = [
                attended[part * rows + side * half : part * rows + (side + 1) * half]
                for part in range(2)
            ]
            vel_out[q_pair * 2 + side] = nt_dot(final, jnp.concatenate(own, axis=0)).astype(BF16)
        if turn < chain - 1:
            for side in range(2):
                vel_copy(q_pair, side).start()
        else:
            vel_copy(z, 1 - core).start()
    vel_in[seq] = vel_out[seq]

    def vel_arrival(hop, carry):
        source = lax.rem(seq + hop, n_seq)
        pltpu.make_async_remote_copy(
            src_ref=vel_out.at[source],
            dst_ref=vel_in.at[source],
            send_sem=vel_send.at[source],
            recv_sem=vel_recv.at[source],
            device_id=(source, blk),
            device_id_type=MESH,
        ).wait_recv()
        return carry

    lax.fori_loop(1, n_seq, vel_arrival, 0)
    velocity = vel_in[0].astype(F32)
    for source in range(1, n_seq):
        velocity = velocity + vel_in[source].astype(F32)
    patch = noisy_ref.shape[0]
    latent = ((noisy_ref[...] - step_size * velocity) / scale_factor).astype(BF16)
    channel = lax.broadcasted_iota(jnp.int32, (LATENT_CH, patch), 0)
    feature = lax.broadcasted_iota(jnp.int32, (LATENT_CH, patch), 1)
    tile = jnp.zeros((LATENT_CH, TILE_VOX), F32)
    for sub in range(4):
        pick = jnp.where(feature == channel * 4 + sub, 1.0, 0.0).astype(BF16)
        tile = tile + jnp.dot(
            jnp.dot(pick, latent, preferred_element_type=F32).astype(BF16),
            spread[sub],
            preferred_element_type=F32,
        )
    own_tile[...] = tile.astype(BF16)

    n_same = chain * n_blk
    index = z * n_blk + blk
    keep = pltpu.make_async_copy(own_tile, tiles_ref.at[z, core, blk], local_sem.at[0])
    keep.start()

    def tile_copy(hop):
        other = lax.rem(index + hop, n_same)
        return pltpu.make_async_remote_copy(
            src_ref=own_tile,
            dst_ref=tiles_ref.at[z, core, blk],
            send_sem=tile_send.at[hop],
            recv_sem=tile_recv.at[index],
            device_id=(lax.div(other, n_blk) * 2 + core, lax.rem(other, n_blk)),
            device_id_type=MESH,
        )

    def tile_start(hop, carry):
        tile_copy(hop).start()
        return carry

    def tile_arrival(hop, carry):
        source = lax.rem(index + n_same - hop, n_same)
        pltpu.make_async_remote_copy(
            src_ref=own_tile,
            dst_ref=tiles_ref.at[lax.div(source, n_blk), core, lax.rem(source, n_blk)],
            send_sem=tile_send.at[hop],
            recv_sem=tile_recv.at[source],
            device_id=(lax.div(source, n_blk) * 2 + core, lax.rem(source, n_blk)),
            device_id_type=MESH,
        ).wait_recv()
        return carry

    def over_copy(source, from_own):
        slot = tiles_ref.at[lax.div(source, n_blk), core, lax.rem(source, n_blk)]
        return pltpu.make_async_remote_copy(
            src_ref=own_tile if from_own else slot,
            dst_ref=slot,
            send_sem=over_send.at[source],
            recv_sem=over_recv.at[source],
            device_id=(z * 2 + 1 - core, blk),
            device_id_type=MESH,
        )

    def tile_over(hop, carry):
        tile_arrival(hop, carry)
        over_copy(lax.rem(index + n_same - hop, n_same), False).start()
        return carry

    def over_arrival(source, carry):
        slot = tiles_ref.at[lax.div(source, n_blk), 1 - core, lax.rem(source, n_blk)]
        pltpu.make_async_remote_copy(
            src_ref=slot,
            dst_ref=slot,
            send_sem=over_send.at[source],
            recv_sem=over_recv.at[source],
            device_id=(z * 2 + 1 - core, blk),
            device_id_type=MESH,
        ).wait_recv()
        return carry

    lax.fori_loop(1, n_same, tile_start, 0)
    over_copy(index, True).start()

    for part in range(2):
        pl.when(z > 0)(lambda: go_left(None, part).wait_send())
        pl.when(z < chain - 1)(lambda: go_right(None, part).wait_send())
        go_over(None, part).wait_send()

        def settle(origin, side):
            if side == "left":
                pl.when(z < chain - 1)(lambda: go_right(origin, part).wait_send())
            else:
                pl.when(z > 0)(lambda: go_left(origin, part).wait_send())
            go_over(origin, part).wait_send()

        for step in range(1, chain):
            each_of_step(step, settle)

    def settle_kv(origin, carry):
        for part in range(2):
            for hop in range(1, n_blk):
                kv_copy(origin, part, hop).wait_send()
        return carry

    lax.fori_loop(0, chain, settle_kv, 0)
    for copy in keeps:
        copy.wait()

    def settle_vel(hop, carry):
        other = lax.rem(seq + hop, n_seq)
        vel_copy(lax.div(other, 2), lax.rem(other, 2)).wait_send()
        return carry

    lax.fori_loop(1, n_seq, settle_vel, 0)

    keep.wait()
    lax.fori_loop(1, n_same, tile_over, 0)

    def settle_tile(hop, carry):
        tile_copy(hop).wait_send()
        over_copy(lax.rem(index + n_same - hop, n_same), False).wait_send()
        return carry

    lax.fori_loop(1, n_same, settle_tile, 0)
    over_copy(index, True).wait_send()
    lax.fori_loop(0, n_same, over_arrival, 0)


def latent_tiles(
    n_seq, n_blk, tokens, project_weight, noisy_latent, final_weight, conv_weight, gain, shift
):
    chain = n_seq // 2
    rows, depth = tokens.shape
    width = project_weight.shape[2]
    channels = conv_weight.shape[1]
    heads = width // HEAD_DIM
    pair = 2 * rows
    dma = pltpu.SemaphoreType.DMA
    vmem = pl.BlockSpec(memory_space=pltpu.VMEM)
    hbm = pl.BlockSpec(memory_space=pl.ANY)
    kept = [
        ((channels, TAPS), BF16),
        ((channels, 2 * TAPS), BF16),
        ((channels, 128), F32),
        ((TILE_VOX, TILE_VOX), BF16),
    ]
    return pl.pallas_call(
        functools.partial(attention_kernel, chain, n_blk),
        out_shape=[jax.ShapeDtypeStruct((chain, 2, n_blk, LATENT_CH, TILE_VOX), BF16)]
        + [jax.ShapeDtypeStruct(*one) for one in kept],
        in_specs=[hbm, hbm] + [vmem] * 5,
        out_specs=[hbm] * 5,
        scratch_shapes=[
            pltpu.VMEM((chain, 2, 2, rows // 2, depth), BF16),
            pltpu.VMEM(project_weight.shape, BF16),
            pltpu.VMEM((chain, pair, width), BF16),
            pltpu.VMEM((chain, 2, 2, n_blk * rows, width), BF16),
            pltpu.VMEM((chain, heads, pair, 2 * HEAD_DIM), F32),
            pltpu.VMEM((chain, heads, pair, HEAD_DIM), F32),
            pltpu.VMEM((n_seq, noisy_latent.shape[0], rows), BF16),
            pltpu.VMEM((n_seq, noisy_latent.shape[0], rows), BF16),
            pltpu.VMEM((LATENT_CH, TILE_VOX), BF16),
            pltpu.VMEM((4, rows, TILE_VOX), BF16),
        ]
        + [pltpu.VMEM(*one) for one in kept]
        + [
            dma((3,)),
            dma((4,)),
            dma((chain, 2, 3)),
            dma((chain, 2, 2)),
            dma((chain, 2, n_blk)),
            dma((chain, 2, n_blk)),
            dma((n_seq,)),
            dma((n_seq,)),
            dma((chain * n_blk,)),
            dma((chain * n_blk,)),
            dma((chain * n_blk,)),
            dma((chain * n_blk,)),
        ],
        compiler_params=pltpu.CompilerParams(
            collective_id=0, has_side_effects=True, vmem_limit_bytes=60 * 2**20
        ),
        name="attention_to_tiles",
    )(tokens, project_weight, noisy_latent, final_weight, conv_weight, gain, shift)


def decode_kernel(
    n_blk,
    count_ref,
    inter_ref,
    tiles_ref,
    weight_first,
    weight_second,
    affine,
    place,
    out_ref,
    patches,
    upper_early,
    upper_late,
    lower_early,
    lower_late,
):
    slot = pl.program_id(0)
    rank = lax.axis_index("seq") * n_blk + lax.axis_index("blk")
    channels = weight_first.shape[0]
    some_ch = channels // 2
    group = channels // GROUPS
    half_vox = TILE_VOX // TILE_F
    inv = 1.0 / (group * TILE_F * FRAME)

    def gather():
        first = lax.fori_loop(0, rank, lambda i, total: total + count_ref[i], 0)
        stack = []
        for number in range(MAXPIX):
            pixel = jnp.minimum(first + number, inter_ref.shape[1] - 1)
            pieces = [tiles_ref[inter_ref[k, pixel]] for k in range(4)]
            for side in range(2):
                for frame in range(TILE_F):
                    lanes = slice(frame * half_vox, (frame + 1) * half_vox)
                    stack.append(
                        jnp.concatenate(
                            [pieces[2 * side][:, lanes], pieces[2 * side + 1][:, lanes]], axis=1
                        )
                    )
        strips = jnp.dot(jnp.concatenate(stack, axis=0), place[...], preferred_element_type=F32)
        held = TILE_F * LATENT_CH
        for number in range(MAXPIX):
            base = number * 2 * held
            region = jnp.concatenate(
                [strips[base : base + held], strips[base + held : base + 2 * held]], axis=1
            )
            lane = lax.broadcasted_iota(jnp.int32, region.shape, 1)
            column = lane & (REGION_COLS - 1)
            row = lane >> 5
            by_row = [
                jnp.where(row == 0, region, pltpu.roll(region, REGION_COLS, 1)),
                region,
                jnp.where(
                    row == REGION_ROWS - 1, region, pltpu.roll(region, FRAME - REGION_COLS, 1)
                ),
            ]
            for b in range(3):
                moved = by_row[b]
                by_col = [
                    jnp.where(column == 0, moved, pltpu.roll(moved, 1, 1)),
                    moved,
                    jnp.where(column == REGION_COLS - 1, moved, pltpu.roll(moved, FRAME - 1, 1)),
                ]
                for g in range(3):
                    tap = by_col[g].astype(BF16)
                    for frame in range(TILE_F):
                        start = frame * TAPS + (b * 3 + g) * LATENT_CH
                        patches[number, pl.ds(start, LATENT_CH), :] = tap[
                            frame * LATENT_CH : (frame + 1) * LATENT_CH
                        ]

    def convolve(number, side, early, late):
        some = pl.ds(side * some_ch, some_ch)
        early[...] = jnp.dot(
            weight_first[some, :], patches[number, :TAPS, :], preferred_element_type=F32
        )
        late[...] = jnp.dot(weight_second[some, :], patches[number], preferred_element_type=F32)

    def finish(side, early, late):
        parts = [x[...].reshape(some_ch // group, group, FRAME) for x in (early, late)]
        mean = jnp.sum(parts[0] + parts[1], axis=(1, 2), keepdims=True) * inv
        spread = jnp.square(parts[0] - mean) + jnp.square(parts[1] - mean)
        var = jnp.sum(spread, axis=(1, 2), keepdims=True) * inv
        both = affine[pl.ds(side * some_ch, some_ch), :]
        gain = both[:, 0:1].reshape(some_ch // group, group, 1)
        shift = both[:, 1:2].reshape(some_ch // group, group, 1)
        slope = 0.5 * gain * lax.rsqrt(var + norm_eps)
        offset = 0.5 * shift - mean * slope
        filled = slot < count_ref[rank]
        slope = jnp.where(filled, slope, 0.0)
        offset = jnp.where(filled, offset, 0.0)
        for frame in range(TILE_F):
            half = parts[frame] * slope + offset
            value = half + half * jnp.tanh(half)
            out_ref[0, 0, pl.ds(side * some_ch, some_ch), pl.ds(frame * FRAME, FRAME)] = (
                value.reshape(some_ch, FRAME).astype(BF16)
            )

    @pl.when(slot == 0)
    def begin():
        gather()
        convolve(0, 0, upper_early, upper_late)

    convolve(slot, 1, lower_early, lower_late)
    finish(0, upper_early, upper_late)
    convolve(jnp.minimum(slot + 1, MAXPIX - 1), 0, upper_early, upper_late)
    finish(1, lower_early, lower_late)


def decode(n_blk, tiles, prepared, owner_count, intersection):
    channels = prepared[0].shape[0]
    voxels = TILE_F * FRAME
    whole = lambda x: pl.BlockSpec(x.shape, lambda i, *_: (0,) * x.ndim)
    return pl.pallas_call(
        functools.partial(decode_kernel, n_blk),
        out_shape=jax.ShapeDtypeStruct((1, MAXPIX, channels, voxels), BF16),
        grid_spec=pltpu.PrefetchScalarGridSpec(
            num_scalar_prefetch=2,
            grid=(MAXPIX,),
            in_specs=[whole(tiles)] + [whole(x) for x in prepared],
            out_specs=pl.BlockSpec((1, 1, channels, voxels), lambda i, *_: (0, i, 0, 0)),
            scratch_shapes=[pltpu.VMEM((MAXPIX, 2 * TAPS, FRAME), BF16)]
            + [pltpu.VMEM((channels // 2, FRAME), F32)] * 4,
        ),
        compiler_params=pltpu.CompilerParams(vmem_limit_bytes=60 * 2**20),
        name="decode_tiles",
    )(owner_count, intersection.T, tiles, *prepared)


def body(
    n_seq,
    n_blk,
    tokens,
    project_weight,
    noisy_latent,
    final_weight,
    conv_weight,
    norm_gain,
    norm_shift,
    owner_count,
    intersection,
):
    tiles, *prepared = latent_tiles(
        n_seq,
        n_blk,
        tokens,
        project_weight,
        noisy_latent.T,
        final_weight.T,
        conv_weight,
        norm_gain.reshape(1, -1),
        norm_shift.reshape(1, -1),
    )
    tiles = tiles.reshape(-1, LATENT_CH, TILE_VOX)
    return decode(n_blk, tiles, prepared, owner_count, intersection)


def solution(mesh):
    return jax.shard_map(
        functools.partial(body, mesh.shape["seq"], mesh.shape["blk"]),
        mesh=mesh,
        in_specs=(
            P(("seq", "blk"), None),
            P(None, None, "seq"),
            P(("seq", "blk"), None),
            P(),
            P(),
            P(),
            P(),
            P(),
            P(),
        ),
        out_specs=P(("seq", "blk"), None, None, None),
        check_vma=False,
    )
```

```python
import functools
import math

import jax
import jax.numpy as jnp
from jax import lax
from jax.experimental import pallas as pl
from jax.experimental.pallas import tpu as pltpu
from jax.sharding import PartitionSpec as P

HEAD_DIM = 128
LATENT_CH = 16
GROUPS = 32
TILE_F = 2
TILE_PH = 8
TILE_PW = 8
MAXPIX = 4

scale_factor = 0.476986
step_size = 0.25
norm_eps = 1e-06

REGION_ROWS = 4 * TILE_PH
REGION_COLS = 4 * TILE_PW
FRAME = REGION_ROWS * REGION_COLS
TAPS = 9 * LATENT_CH
MESH = pl.DeviceIdType.MESH
F32 = jnp.float32
BF16 = jnp.bfloat16
TILE_VOX = TILE_F * 4 * TILE_PH * TILE_PW


def nt_dot(a, b):
    return lax.dot_general(a, b, (((1,), (1,)), ((), ())), preferred_element_type=F32)


def attention_kernel(
    chain,
    n_blk,
    tokens_ref,
    weight_ref,
    noisy_ref,
    final_ref,
    conv_ref,
    gain_ref,
    shift_ref,
    tiles_ref,
    first_ref,
    second_ref,
    affine_ref,
    place_ref,
    tok,
    weight,
    q_all,
    kv_all,
    acc_all,
    max_all,
    vel_out,
    vel_in,
    own_tile,
    spread,
    first,
    second,
    affine,
    place,
    local_sem,
    keep_sem,
    tok_send,
    tok_recv,
    kv_send,
    kv_recv,
    vel_send,
    vel_recv,
    tile_send,
    tile_recv,
    over_send,
    over_recv,
):
    n_seq = 2 * chain
    seq = lax.axis_index("seq")
    blk = lax.axis_index("blk")
    z = lax.div(seq, 2)
    core = lax.rem(seq, 2)
    me = seq * n_blk + blk
    rows = tokens_ref.shape[0]
    half = rows // 2
    width = q_all.shape[2]
    heads = width // HEAD_DIM

    load_weight = pltpu.make_async_copy(weight_ref, weight, local_sem.at[0])
    load_weight.start()
    load_tokens = []
    for part in range(2):
        load_tokens.append(
            pltpu.make_async_copy(
                tokens_ref.at[pl.ds(part * half, half)],
                tok.at[z, part, core],
                local_sem.at[1 + part],
            )
        )
        load_tokens[part].start()

    barrier = pltpu.get_barrier_semaphore()

    def greet(target_seq, target_blk):
        pl.semaphore_signal(
            barrier, inc=1, device_id=(target_seq, target_blk), device_id_type=MESH
        )

    greet(seq + 1 - 2 * core, blk)
    pl.when(z > 0)(lambda: greet(seq - 2, blk))
    pl.when(z < chain - 1)(lambda: greet(seq + 2, blk))
    for hop in range(1, n_blk):
        greet(seq, lax.rem(blk + hop, n_blk))
    ends = jnp.where(z > 0, 1, 0) + jnp.where(z < chain - 1, 1, 0)
    pl.semaphore_wait(barrier, n_blk + ends)

    def tok_copy(origin, part, side, target_z, target_core):
        if origin is None:
            origin, source = z, tokens_ref.at[pl.ds(part * half, half)]
        else:
            source = tok.at[origin, part, core]
        return pltpu.make_async_remote_copy(
            src_ref=source,
            dst_ref=tok.at[origin, part, core],
            send_sem=tok_send.at[origin, part, side],
            recv_sem=tok_recv.at[origin, part, core],
            device_id=(target_z * 2 + target_core, blk),
            device_id_type=MESH,
        )

    def tok_arrival(origin, part, origin_core):
        pltpu.make_async_remote_copy(
            src_ref=tok.at[origin, part, origin_core],
            dst_ref=tok.at[origin, part, origin_core],
            send_sem=tok_send.at[origin, part, 0],
            recv_sem=tok_recv.at[origin, part, origin_core],
            device_id=(z * 2 + 1 - core, blk),
            device_id_type=MESH,
        ).wait_recv()

    def go_left(origin, part):
        return tok_copy(origin, part, 0, z - 1, core)

    def go_right(origin, part):
        return tok_copy(origin, part, 1, z + 1, core)

    def go_over(origin, part):
        return tok_copy(origin, part, 2, z, 1 - core)

    def kv_place(origin, part, source):
        return kv_all.at[origin, part, :, pl.ds(pl.multiple_of(source * rows, rows), rows), :]

    def kv_copy(origin, part, hop):
        return pltpu.make_async_remote_copy(
            src_ref=kv_place(origin, part, blk),
            dst_ref=kv_place(origin, part, blk),
            send_sem=kv_send.at[origin, part, hop],
            recv_sem=kv_recv.at[origin, part, blk],
            device_id=(seq, lax.rem(blk + hop, n_blk)),
            device_id_type=MESH,
        )

    def kv_arrival(origin, part, hop):
        source = lax.rem(blk + n_blk - hop, n_blk)
        pltpu.make_async_remote_copy(
            src_ref=kv_place(origin, part, source),
            dst_ref=kv_place(origin, part, source),
            send_sem=kv_send.at[origin, part, hop],
            recv_sem=kv_recv.at[origin, part, source],
            device_id=(seq, lax.rem(blk + hop, n_blk)),
            device_id_type=MESH,
        ).wait_recv()

    def project(origin, part):
        x = tok[origin, part].reshape(rows, tok.shape[4])
        own = pl.ds(pl.multiple_of(blk * rows, rows), rows)
        for kind in range(2):
            kv_all[origin, part, kind, own, :] = jnp.dot(
                x, weight[kind + 1], preferred_element_type=F32
            ).astype(BF16)
        for hop in range(1, n_blk):
            kv_copy(origin, part, hop).start()
        query = jnp.dot(x, weight[0], preferred_element_type=F32)
        query = (query * (HEAD_DIM**-0.5 * math.log2(math.e))).astype(BF16)
        some = pl.ds(part * rows, rows)
        q_all[origin, some, :] = query
        for head in range(heads):
            max_all[origin, head, some, :] = jnp.full((rows, HEAD_DIM), -1e30, F32)
            acc_all[origin, head, some, :] = jnp.zeros((rows, 2 * HEAD_DIM), F32)

    def attend(q_pair, kv_pair, part):
        every = range(heads)
        lanes = [pl.ds(head * HEAD_DIM, HEAD_DIM) for head in every]
        scores = [
            nt_dot(q_all[q_pair, :, lanes[h]], kv_all[kv_pair, part, 0, :, lanes[h]])
            for h in every
        ]
        values = [kv_all[kv_pair, part, 1, :, lanes[h]] for h in every]
        old_max = [max_all[q_pair, h] for h in every]
        old_acc = [acc_all[q_pair, h] for h in every]
        new_max = [
            jnp.maximum(old_max[h], jnp.max(scores[h], axis=1, keepdims=True)) for h in every
        ]
        rescale = [jnp.exp2(old_max[h] - new_max[h]) for h in every]
        weights = [jnp.exp2(scores[h] - new_max[h][:, :1]).astype(BF16) for h in every]
        product = [
            jnp.dot(
                weights[h],
                jnp.concatenate([values[h], jnp.ones_like(values[h])], axis=1),
                preferred_element_type=F32,
            )
            for h in every
        ]
        for h in every:
            wide = jnp.concatenate([rescale[h], rescale[h]], axis=1)
            acc_all[q_pair, h] = old_acc[h] * wide + product[h]
            max_all[q_pair, h] = new_max[h]

    def each_of_step(step, action):
        if step >= chain:
            return
        if step == 0:
            action(z, None)
            return
        pl.when(z - step >= 0)(lambda: action(z - step, "left"))
        pl.when(z + step < chain)(lambda: action(z + step, "right"))

    def over_known(radius, action):
        low = jnp.maximum(z - radius, 0)
        high = jnp.minimum(z + radius, chain - 1) + 1

        def one(index, carry):
            action(index)
            return carry

        lax.fori_loop(low, high, one, 0)

    def forward(part):
        def action(origin, side):
            tok_arrival(origin, part, core)
            if side == "left":
                pl.when(z < chain - 1)(lambda: go_right(origin, part).start())
            else:
                pl.when(z > 0)(lambda: go_left(origin, part).start())
            go_over(origin, part).start()

        return action

    def project_arrived(part):
        def action(origin, side):
            tok_arrival(origin, part, 1 - core)
            project(origin, part)

        return action

    for part in range(2):
        pl.when(z > 0)(lambda: go_left(None, part).start())
        pl.when(z < chain - 1)(lambda: go_right(None, part).start())
        go_over(None, part).start()

    def prepare():
        token = lax.broadcasted_iota(jnp.int32, (rows, TILE_VOX), 0)
        voxel = lax.broadcasted_iota(jnp.int32, (rows, TILE_VOX), 1)
        row, column = (voxel >> 4) & 15, voxel & 15
        home = (voxel >> 8) * (TILE_PH * TILE_PW) + (row >> 1) * TILE_PW + (column >> 1)
        for sub in range(4):
            hit = (home == token) & ((row & 1) * 2 + (column & 1) == sub)
            spread[sub] = jnp.where(hit, 1.0, 0.0).astype(BF16)
        taps = [conv_ref[pl.ds(a * TAPS, TAPS), :].astype(F32) for a in range(3)]
        early = taps[0] + taps[1]
        first[...] = (early + taps[2]).T.astype(BF16)
        second[...] = jnp.concatenate([early, taps[2]], axis=0).T.astype(BF16)
        channels = conv_ref.shape[1]
        index = lax.broadcasted_iota(jnp.int32, (128, channels), 0)
        affine[...] = jnp.where(index == 0, gain_ref[...], shift_ref[...]).T
        source = lax.broadcasted_iota(jnp.int32, place.shape, 0)
        target = lax.broadcasted_iota(jnp.int32, place.shape, 1)
        wanted = ((source >> 4) & 15) * REGION_COLS + (source >> 8) * 16 + (source & 15)
        place[...] = jnp.where(wanted == target, 1.0, 0.0).astype(BF16)
        for copy in keeps:
            copy.start()

    keeps = [
        pltpu.make_async_copy(source, target, keep_sem.at[number])
        for number, (source, target) in enumerate(
            [(first, first_ref), (second, second_ref), (affine, affine_ref), (place, place_ref)]
        )
    ]

    load_weight.wait()
    load_tokens[0].wait()
    load_tokens[1].wait()
    for part in range(2):
        project_arrived(part)(z, None)

    def attend_both(q_pair, kv_pair):
        attend(q_pair, kv_pair, 0)
        attend(q_pair, kv_pair, 1)

    for turn in range(2 * chain):
        step, part = turn // 2, turn % 2
        if turn >= 1:
            each_of_step((turn + 1) // 2, forward((turn + 1) % 2))
            each_of_step((turn + 1) // 2, project_arrived((turn + 1) % 2))
        if turn == 0:
            prepare()
        if part == 0 and step >= 1:
            each_of_step(
                step, lambda o, side: over_known(step - 1, lambda other: attend_both(o, other))
            )

        def meet(origin, side):
            for hop in range(1, n_blk):
                kv_arrival(origin, part, hop)
            if turn < 2 * chain - 1:
                over_known(step, lambda other: attend(other, origin, part))

        each_of_step(step, meet)

    final = final_ref[:, pl.ds(pl.multiple_of(seq * width, width), width)]

    def vel_copy(target_z, target_core):
        target = target_z * 2 + target_core
        return pltpu.make_async_remote_copy(
            src_ref=vel_out.at[target],
            dst_ref=vel_in.at[seq],
            send_sem=vel_send.at[target],
            recv_sem=vel_recv.at[seq],
            device_id=(target, blk),
            device_id_type=MESH,
        )

    for turn in range(chain):
        q_pair = lax.rem(z + 1 + turn, chain)
        pl.when((z == 0) | (z == chain - 1))(lambda: attend(q_pair, chain - 1 - z, 1))
        attended = []
        for head in range(heads):
            total = acc_all[q_pair, head]
            attended.append((total[:, :HEAD_DIM] / total[:, HEAD_DIM:]).astype(BF16))
        attended = jnp.concatenate(attended, axis=1)
        for side in range(2):
            own = [
                attended[part * rows + side * half : part * rows + (side + 1) * half]
                for part in range(2)
            ]
            vel_out[q_pair * 2 + side] = nt_dot(final, jnp.concatenate(own, axis=0)).astype(BF16)
        if turn < chain - 1:
            for side in range(2):
                vel_copy(q_pair, side).start()
        else:
            vel_copy(z, 1 - core).start()
    vel_in[seq] = vel_out[seq]

    def vel_arrival(hop, carry):
        source = lax.rem(seq + hop, n_seq)
        pltpu.make_async_remote_copy(
            src_ref=vel_out.at[source],
            dst_ref=vel_in.at[source],
            send_sem=vel_send.at[source],
            recv_sem=vel_recv.at[source],
            device_id=(source, blk),
            device_id_type=MESH,
        ).wait_recv()
        return carry

    lax.fori_loop(1, n_seq, vel_arrival, 0)
    velocity = vel_in[0].astype(F32)
    for source in range(1, n_seq):
        velocity = velocity + vel_in[source].astype(F32)
    patch = noisy_ref.shape[0]
    latent = ((noisy_ref[...] - step_size * velocity) / scale_factor).astype(BF16)
    channel = lax.broadcasted_iota(jnp.int32, (LATENT_CH, patch), 0)
    feature = lax.broadcasted_iota(jnp.int32, (LATENT_CH, patch), 1)
    tile = jnp.zeros((LATENT_CH, TILE_VOX), F32)
    for sub in range(4):
        pick = jnp.where(feature == channel * 4 + sub, 1.0, 0.0).astype(BF16)
        tile = tile + jnp.dot(
            jnp.dot(pick, latent, preferred_element_type=F32).astype(BF16),
            spread[sub],
            preferred_element_type=F32,
        )
    own_tile[...] = tile.astype(BF16)

    n_same = chain * n_blk
    index = z * n_blk + blk
    keep = pltpu.make_async_copy(own_tile, tiles_ref.at[z, core, blk], local_sem.at[0])
    keep.start()

    def tile_copy(hop):
        other = lax.rem(index + hop, n_same)
        return pltpu.make_async_remote_copy(
            src_ref=own_tile,
            dst_ref=tiles_ref.at[z, core, blk],
            send_sem=tile_send.at[hop],
            recv_sem=tile_recv.at[index],
            device_id=(lax.div(other, n_blk) * 2 + core, lax.rem(other, n_blk)),
            device_id_type=MESH,
        )

    def tile_start(hop, carry):
        tile_copy(hop).start()
        return carry

    def tile_arrival(hop, carry):
        source = lax.rem(index + n_same - hop, n_same)
        pltpu.make_async_remote_copy(
            src_ref=own_tile,
            dst_ref=tiles_ref.at[lax.div(source, n_blk), core, lax.rem(source, n_blk)],
            send_sem=tile_send.at[hop],
            recv_sem=tile_recv.at[source],
            device_id=(lax.div(source, n_blk) * 2 + core, lax.rem(source, n_blk)),
            device_id_type=MESH,
        ).wait_recv()
        return carry

    def over_copy(source, from_own):
        slot = tiles_ref.at[lax.div(source, n_blk), core, lax.rem(source, n_blk)]
        return pltpu.make_async_remote_copy(
            src_ref=own_tile if from_own else slot,
            dst_ref=slot,
            send_sem=over_send.at[source],
            recv_sem=over_recv.at[source],
            device_id=(z * 2 + 1 - core, blk),
            device_id_type=MESH,
        )

    def tile_over(hop, carry):
        tile_arrival(hop, carry)
        over_copy(lax.rem(index + n_same - hop, n_same), False).start()
        return carry

    def over_arrival(source, carry):
        slot = tiles_ref.at[lax.div(source, n_blk), 1 - core, lax.rem(source, n_blk)]
        pltpu.make_async_remote_copy(
            src_ref=slot,
            dst_ref=slot,
            send_sem=over_send.at[source],
            recv_sem=over_recv.at[source],
            device_id=(z * 2 + 1 - core, blk),
            device_id_type=MESH,
        ).wait_recv()
        return carry

    lax.fori_loop(1, n_same, tile_start, 0)
    over_copy(index, True).start()

    for part in range(2):
        pl.when(z > 0)(lambda: go_left(None, part).wait_send())
        pl.when(z < chain - 1)(lambda: go_right(None, part).wait_send())
        go_over(None, part).wait_send()

        def settle(origin, side):
            if side == "left":
                pl.when(z < chain - 1)(lambda: go_right(origin, part).wait_send())
            else:
                pl.when(z > 0)(lambda: go_left(origin, part).wait_send())
            go_over(origin, part).wait_send()

        for step in range(1, chain):
            each_of_step(step, settle)

    def settle_kv(origin, carry):
        for part in range(2):
            for hop in range(1, n_blk):
                kv_copy(origin, part, hop).wait_send()
        return carry

    lax.fori_loop(0, chain, settle_kv, 0)
    for copy in keeps:
        copy.wait()

    def settle_vel(hop, carry):
        other = lax.rem(seq + hop, n_seq)
        vel_copy(lax.div(other, 2), lax.rem(other, 2)).wait_send()
        return carry

    lax.fori_loop(1, n_seq, settle_vel, 0)

    keep.wait()
    lax.fori_loop(1, n_same, tile_over, 0)

    def settle_tile(hop, carry):
        tile_copy(hop).wait_send()
        over_copy(lax.rem(index + n_same - hop, n_same), False).wait_send()
        return carry

    lax.fori_loop(1, n_same, settle_tile, 0)
    over_copy(index, True).wait_send()
    lax.fori_loop(0, n_same, over_arrival, 0)


def latent_tiles(
    n_seq, n_blk, tokens, project_weight, noisy_latent, final_weight, conv_weight, gain, shift
):
    chain = n_seq // 2
    rows, depth = tokens.shape
    width = project_weight.shape[2]
    channels = conv_weight.shape[1]
    heads = width // HEAD_DIM
    pair = 2 * rows
    dma = pltpu.SemaphoreType.DMA
    vmem = pl.BlockSpec(memory_space=pltpu.VMEM)
    hbm = pl.BlockSpec(memory_space=pl.ANY)
    kept = [
        ((channels, TAPS), BF16),
        ((channels, 2 * TAPS), BF16),
        ((channels, 128), F32),
        ((TILE_VOX, TILE_VOX), BF16),
    ]
    return pl.pallas_call(
        functools.partial(attention_kernel, chain, n_blk),
        out_shape=[jax.ShapeDtypeStruct((chain, 2, n_blk, LATENT_CH, TILE_VOX), BF16)]
        + [jax.ShapeDtypeStruct(*one) for one in kept],
        in_specs=[hbm, hbm] + [vmem] * 5,
        out_specs=[hbm] * 5,
        scratch_shapes=[
            pltpu.VMEM((chain, 2, 2, rows // 2, depth), BF16),
            pltpu.VMEM(project_weight.shape, BF16),
            pltpu.VMEM((chain, pair, width), BF16),
            pltpu.VMEM((chain, 2, 2, n_blk * rows, width), BF16),
            pltpu.VMEM((chain, heads, pair, 2 * HEAD_DIM), F32),
            pltpu.VMEM((chain, heads, pair, HEAD_DIM), F32),
            pltpu.VMEM((n_seq, noisy_latent.shape[0], rows), BF16),
            pltpu.VMEM((n_seq, noisy_latent.shape[0], rows), BF16),
            pltpu.VMEM((LATENT_CH, TILE_VOX), BF16),
            pltpu.VMEM((4, rows, TILE_VOX), BF16),
        ]
        + [pltpu.VMEM(*one) for one in kept]
        + [
            dma((3,)),
            dma((4,)),
            dma((chain, 2, 3)),
            dma((chain, 2, 2)),
            dma((chain, 2, n_blk)),
            dma((chain, 2, n_blk)),
            dma((n_seq,)),
            dma((n_seq,)),
            dma((chain * n_blk,)),
            dma((chain * n_blk,)),
            dma((chain * n_blk,)),
            dma((chain * n_blk,)),
        ],
        compiler_params=pltpu.CompilerParams(
            collective_id=0, has_side_effects=True, vmem_limit_bytes=60 * 2**20
        ),
        name="attention_to_tiles",
    )(tokens, project_weight, noisy_latent, final_weight, conv_weight, gain, shift)


def decode_kernel(
    n_blk,
    count_ref,
    inter_ref,
    tiles_ref,
    weight_first,
    weight_second,
    affine,
    place,
    out_ref,
    patches,
    upper_early,
    upper_late,
    lower_early,
    lower_late,
):
    slot = pl.program_id(0)
    rank = lax.axis_index("seq") * n_blk + lax.axis_index("blk")
    channels = weight_first.shape[0]
    some_ch = channels // 2
    group = channels // GROUPS
    half_vox = TILE_VOX // TILE_F
    inv = 1.0 / (group * TILE_F * FRAME)

    def gather():
        first = lax.fori_loop(0, rank, lambda i, total: total + count_ref[i], 0)
        stack = []
        for number in range(MAXPIX):
            pixel = jnp.minimum(first + number, inter_ref.shape[1] - 1)
            pieces = [tiles_ref[inter_ref[k, pixel]] for k in range(4)]
            for side in range(2):
                for frame in range(TILE_F):
                    lanes = slice(frame * half_vox, (frame + 1) * half_vox)
                    stack.append(
                        jnp.concatenate(
                            [pieces[2 * side][:, lanes], pieces[2 * side + 1][:, lanes]], axis=1
                        )
                    )
        strips = jnp.dot(jnp.concatenate(stack, axis=0), place[...], preferred_element_type=F32)
        held = TILE_F * LATENT_CH
        for number in range(MAXPIX):
            base = number * 2 * held
            region = jnp.concatenate(
                [strips[base : base + held], strips[base + held : base + 2 * held]], axis=1
            )
            lane = lax.broadcasted_iota(jnp.int32, region.shape, 1)
            column = lane & (REGION_COLS - 1)
            row = lane >> 5
            by_row = [
                jnp.where(row == 0, region, pltpu.roll(region, REGION_COLS, 1)),
                region,
                jnp.where(
                    row == REGION_ROWS - 1, region, pltpu.roll(region, FRAME - REGION_COLS, 1)
                ),
            ]
            for b in range(3):
                moved = by_row[b]
                by_col = [
                    jnp.where(column == 0, moved, pltpu.roll(moved, 1, 1)),
                    moved,
                    jnp.where(column == REGION_COLS - 1, moved, pltpu.roll(moved, FRAME - 1, 1)),
                ]
                for g in range(3):
                    tap = by_col[g].astype(BF16)
                    for frame in range(TILE_F):
                        start = frame * TAPS + (b * 3 + g) * LATENT_CH
                        patches[number, pl.ds(start, LATENT_CH), :] = tap[
                            frame * LATENT_CH : (frame + 1) * LATENT_CH
                        ]

    def convolve(number, side, early, late):
        some = pl.ds(side * some_ch, some_ch)
        early[...] = jnp.dot(
            weight_first[some, :], patches[number, :TAPS, :], preferred_element_type=F32
        )
        late[...] = jnp.dot(weight_second[some, :], patches[number], preferred_element_type=F32)

    def finish(side, early, late):
        parts = [x[...].reshape(some_ch // group, group, FRAME) for x in (early, late)]
        mean = jnp.sum(parts[0] + parts[1], axis=(1, 2), keepdims=True) * inv
        spread = jnp.square(parts[0] - mean) + jnp.square(parts[1] - mean)
        var = jnp.sum(spread, axis=(1, 2), keepdims=True) * inv
        both = affine[pl.ds(side * some_ch, some_ch), :]
        gain = both[:, 0:1].reshape(some_ch // group, group, 1)
        shift = both[:, 1:2].reshape(some_ch // group, group, 1)
        slope = 0.5 * gain * lax.rsqrt(var + norm_eps)
        offset = 0.5 * shift - mean * slope
        filled = slot < count_ref[rank]
        slope = jnp.where(filled, slope, 0.0)
        offset = jnp.where(filled, offset, 0.0)
        for frame in range(TILE_F):
            half = parts[frame] * slope + offset
            value = half + half * jnp.tanh(half)
            out_ref[0, 0, pl.ds(side * some_ch, some_ch), pl.ds(frame * FRAME, FRAME)] = (
                value.reshape(some_ch, FRAME).astype(BF16)
            )

    @pl.when(slot == 0)
    def begin():
        gather()
        convolve(0, 0, upper_early, upper_late)

    convolve(slot, 1, lower_early, lower_late)
    finish(0, upper_early, upper_late)
    convolve(jnp.minimum(slot + 1, MAXPIX - 1), 0, upper_early, upper_late)
    finish(1, lower_early, lower_late)


def decode(n_blk, tiles, prepared, owner_count, intersection):
    channels = prepared[0].shape[0]
    voxels = TILE_F * FRAME
    whole = lambda x: pl.BlockSpec(x.shape, lambda i, *_: (0,) * x.ndim)
    return pl.pallas_call(
        functools.partial(decode_kernel, n_blk),
        out_shape=jax.ShapeDtypeStruct((1, MAXPIX, channels, voxels), BF16),
        grid_spec=pltpu.PrefetchScalarGridSpec(
            num_scalar_prefetch=2,
            grid=(MAXPIX,),
            in_specs=[whole(tiles)] + [whole(x) for x in prepared],
            out_specs=pl.BlockSpec((1, 1, channels, voxels), lambda i, *_: (0, i, 0, 0)),
            scratch_shapes=[pltpu.VMEM((MAXPIX, 2 * TAPS, FRAME), BF16)]
            + [pltpu.VMEM((channels // 2, FRAME), F32)] * 4,
        ),
        compiler_params=pltpu.CompilerParams(vmem_limit_bytes=60 * 2**20),
        name="decode_tiles",
    )(owner_count, intersection.T, tiles, *prepared)


def body(
    n_seq,
    n_blk,
    tokens,
    project_weight,
    noisy_latent,
    final_weight,
    conv_weight,
    norm_gain,
    norm_shift,
    owner_count,
    intersection,
):
    tiles, *prepared = latent_tiles(
        n_seq,
        n_blk,
        tokens,
        project_weight,
        noisy_latent.T,
        final_weight.T,
        conv_weight,
        norm_gain.reshape(1, -1),
        norm_shift.reshape(1, -1),
    )
    tiles = tiles.reshape(-1, LATENT_CH, TILE_VOX)
    return decode(n_blk, tiles, prepared, owner_count, intersection)


def solution(mesh):
    return jax.shard_map(
        functools.partial(body, mesh.shape["seq"], mesh.shape["blk"]),
        mesh=mesh,
        in_specs=(
            P(("seq", "blk"), None),
            P(None, None, "seq"),
            P(("seq", "blk"), None),
            P(),
            P(),
            P(),
            P(),
            P(),
            P(),
        ),
        out_specs=P(("seq", "blk"), None, None, None),
        check_vma=False,
    )
```

```python
import functools
import math

import jax
import jax.numpy as jnp
from jax import lax
from jax.experimental import pallas as pl
from jax.experimental.pallas import tpu as pltpu
from jax.sharding import PartitionSpec as P

HEAD_DIM = 128
LATENT_CH = 16
GROUPS = 32
TILE_F = 2
TILE_PH = 8
TILE_PW = 8
MAXPIX = 4

scale_factor = 0.476986
step_size = 0.25
norm_eps = 1e-06

REGION_ROWS = 4 * TILE_PH
REGION_COLS = 4 * TILE_PW
FRAME = REGION_ROWS * REGION_COLS
TAPS = 9 * LATENT_CH
MESH = pl.DeviceIdType.MESH
F32 = jnp.float32
BF16 = jnp.bfloat16
TILE_VOX = TILE_F * 4 * TILE_PH * TILE_PW


def nt_dot(a, b):
    return lax.dot_general(a, b, (((1,), (1,)), ((), ())), preferred_element_type=F32)


def attention_kernel(
    chain,
    n_blk,
    tokens_ref,
    weight_ref,
    noisy_ref,
    final_ref,
    conv_ref,
    gain_ref,
    shift_ref,
    tiles_ref,
    first_ref,
    second_ref,
    affine_ref,
    place_ref,
    tok,
    weight,
    q_all,
    kv_all,
    acc_all,
    max_all,
    vel_out,
    vel_in,
    own_tile,
    spread,
    first,
    second,
    affine,
    place,
    local_sem,
    keep_sem,
    tok_send,
    tok_recv,
    kv_send,
    kv_recv,
    vel_send,
    vel_recv,
    tile_send,
    tile_recv,
    over_send,
    over_recv,
):
    n_seq = 2 * chain
    seq = lax.axis_index("seq")
    blk = lax.axis_index("blk")
    z = lax.div(seq, 2)
    core = lax.rem(seq, 2)
    me = seq * n_blk + blk
    rows = tokens_ref.shape[0]
    half = rows // 2
    width = q_all.shape[2]
    heads = width // HEAD_DIM

    load_weight = pltpu.make_async_copy(weight_ref, weight, local_sem.at[0])
    load_weight.start()
    load_tokens = []
    for part in range(2):
        load_tokens.append(
            pltpu.make_async_copy(
                tokens_ref.at[pl.ds(part * half, half)],
                tok.at[z, part, core],
                local_sem.at[1 + part],
            )
        )
        load_tokens[part].start()

    barrier = pltpu.get_barrier_semaphore()

    def greet(target_seq, target_blk):
        pl.semaphore_signal(
            barrier, inc=1, device_id=(target_seq, target_blk), device_id_type=MESH
        )

    greet(seq + 1 - 2 * core, blk)
    pl.when(z > 0)(lambda: greet(seq - 2, blk))
    pl.when(z < chain - 1)(lambda: greet(seq + 2, blk))
    for hop in range(1, n_blk):
        greet(seq, lax.rem(blk + hop, n_blk))
    ends = jnp.where(z > 0, 1, 0) + jnp.where(z < chain - 1, 1, 0)
    pl.semaphore_wait(barrier, n_blk + ends)

    def tok_copy(origin, part, side, target_z, target_core):
        if origin is None:
            origin, source = z, tokens_ref.at[pl.ds(part * half, half)]
        else:
            source = tok.at[origin, part, core]
        return pltpu.make_async_remote_copy(
            src_ref=source,
            dst_ref=tok.at[origin, part, core],
            send_sem=tok_send.at[origin, part, side],
            recv_sem=tok_recv.at[origin, part, core],
            device_id=(target_z * 2 + target_core, blk),
            device_id_type=MESH,
        )

    def tok_arrival(origin, part, origin_core):
        pltpu.make_async_remote_copy(
            src_ref=tok.at[origin, part, origin_core],
            dst_ref=tok.at[origin, part, origin_core],
            send_sem=tok_send.at[origin, part, 0],
            recv_sem=tok_recv.at[origin, part, origin_core],
            device_id=(z * 2 + 1 - core, blk),
            device_id_type=MESH,
        ).wait_recv()

    def go_left(origin, part):
        return tok_copy(origin, part, 0, z - 1, core)

    def go_right(origin, part):
        return tok_copy(origin, part, 1, z + 1, core)

    def go_over(origin, part):
        return tok_copy(origin, part, 2, z, 1 - core)

    def kv_place(origin, part, source):
        return kv_all.at[origin, part, :, pl.ds(pl.multiple_of(source * rows, rows), rows), :]

    def kv_copy(origin, part, hop):
        return pltpu.make_async_remote_copy(
            src_ref=kv_place(origin, part, blk),
            dst_ref=kv_place(origin, part, blk),
            send_sem=kv_send.at[origin, part, hop],
            recv_sem=kv_recv.at[origin, part, blk],
            device_id=(seq, lax.rem(blk + hop, n_blk)),
            device_id_type=MESH,
        )

    def kv_arrival(origin, part, hop):
        source = lax.rem(blk + n_blk - hop, n_blk)
        pltpu.make_async_remote_copy(
            src_ref=kv_place(origin, part, source),
            dst_ref=kv_place(origin, part, source),
            send_sem=kv_send.at[origin, part, hop],
            recv_sem=kv_recv.at[origin, part, source],
            device_id=(seq, lax.rem(blk + hop, n_blk)),
            device_id_type=MESH,
        ).wait_recv()

    def project(origin, part):
        x = tok[origin, part].reshape(rows, tok.shape[4])
        own = pl.ds(pl.multiple_of(blk * rows, rows), rows)
        for kind in range(2):
            kv_all[origin, part, kind, own, :] = jnp.dot(
                x, weight[kind + 1], preferred_element_type=F32
            ).astype(BF16)
        for hop in range(1, n_blk):
            kv_copy(origin, part, hop).start()
        query = jnp.dot(x, weight[0], preferred_element_type=F32)
        query = (query * (HEAD_DIM**-0.5 * math.log2(math.e))).astype(BF16)
        some = pl.ds(part * rows, rows)
        q_all[origin, some, :] = query
        for head in range(heads):
            max_all[origin, head, some, :] = jnp.full((rows, HEAD_DIM), -1e30, F32)
            acc_all[origin, head, some, :] = jnp.zeros((rows, 2 * HEAD_DIM), F32)

    def attend(q_pair, kv_pair, *parts):
        every = range(heads)

        def rows_of(kind, lane):
            pieces = [kv_all[kv_pair, part, kind, :, lane] for part in parts]
            return pieces[0] if len(pieces) == 1 else jnp.concatenate(pieces, axis=0)

        lanes = [pl.ds(head * HEAD_DIM, HEAD_DIM) for head in every]
        scores = [nt_dot(q_all[q_pair, :, lanes[h]], rows_of(0, lanes[h])) for h in every]
        values = [rows_of(1, lanes[h]) for h in every]
        old_max = [max_all[q_pair, h] for h in every]
        old_acc = [acc_all[q_pair, h] for h in every]
        new_max = [
            jnp.maximum(old_max[h], jnp.max(scores[h], axis=1, keepdims=True)) for h in every
        ]
        rescale = [jnp.exp2(old_max[h] - new_max[h]) for h in every]
        weights = [jnp.exp2(scores[h] - new_max[h][:, :1]).astype(BF16) for h in every]
        product = [
            jnp.dot(
                weights[h],
                jnp.concatenate([values[h], jnp.ones_like(values[h])], axis=1),
                preferred_element_type=F32,
            )
            for h in every
        ]
        for h in every:
            wide = jnp.concatenate([rescale[h], rescale[h]], axis=1)
            acc_all[q_pair, h] = old_acc[h] * wide + product[h]
            max_all[q_pair, h] = new_max[h]

    def each_of_step(step, action):
        if step >= chain:
            return
        if step == 0:
            action(z, None)
            return
        pl.when(z - step >= 0)(lambda: action(z - step, "left"))
        pl.when(z + step < chain)(lambda: action(z + step, "right"))

    def over_known(radius, action):
        low = jnp.maximum(z - radius, 0)
        high = jnp.minimum(z + radius, chain - 1) + 1

        def one(index, carry):
            action(index)
            return carry

        lax.fori_loop(low, high, one, 0)

    def forward(part):
        def action(origin, side):
            tok_arrival(origin, part, core)
            if side == "left":
                pl.when(z < chain - 1)(lambda: go_right(origin, part).start())
            else:
                pl.when(z > 0)(lambda: go_left(origin, part).start())
            go_over(origin, part).start()

        return action

    def project_arrived(part):
        def action(origin, side):
            tok_arrival(origin, part, 1 - core)
            project(origin, part)

        return action

    for part in range(2):
        pl.when(z > 0)(lambda: go_left(None, part).start())
        pl.when(z < chain - 1)(lambda: go_right(None, part).start())
        go_over(None, part).start()

    def prepare():
        token = lax.broadcasted_iota(jnp.int32, (rows, TILE_VOX), 0)
        voxel = lax.broadcasted_iota(jnp.int32, (rows, TILE_VOX), 1)
        row, column = (voxel >> 4) & 15, voxel & 15
        home = (voxel >> 8) * (TILE_PH * TILE_PW) + (row >> 1) * TILE_PW + (column >> 1)
        for sub in range(4):
            hit = (home == token) & ((row & 1) * 2 + (column & 1) == sub)
            spread[sub] = jnp.where(hit, 1.0, 0.0).astype(BF16)
        taps = [conv_ref[pl.ds(a * TAPS, TAPS), :].astype(F32) for a in range(3)]
        early = taps[0] + taps[1]
        first[...] = (early + taps[2]).T.astype(BF16)
        second[...] = jnp.concatenate([early, taps[2]], axis=0).T.astype(BF16)
        channels = conv_ref.shape[1]
        index = lax.broadcasted_iota(jnp.int32, (128, channels), 0)
        affine[...] = jnp.where(index == 0, gain_ref[...], shift_ref[...]).T
        source = lax.broadcasted_iota(jnp.int32, place.shape, 0)
        target = lax.broadcasted_iota(jnp.int32, place.shape, 1)
        wanted = ((source >> 4) & 15) * REGION_COLS + (source >> 8) * 16 + (source & 15)
        place[...] = jnp.where(wanted == target, 1.0, 0.0).astype(BF16)
        for copy in keeps:
            copy.start()

    keeps = [
        pltpu.make_async_copy(source, target, keep_sem.at[number])
        for number, (source, target) in enumerate(
            [(first, first_ref), (second, second_ref), (affine, affine_ref), (place, place_ref)]
        )
    ]

    load_weight.wait()
    load_tokens[0].wait()
    load_tokens[1].wait()
    for part in range(2):
        project_arrived(part)(z, None)

    def attend_both(q_pair, kv_pair):
        attend(q_pair, kv_pair, 0, 1)

    for turn in range(2 * chain):
        step, part = turn // 2, turn % 2
        if turn >= 1:
            each_of_step((turn + 1) // 2, forward((turn + 1) % 2))
            each_of_step((turn + 1) // 2, project_arrived((turn + 1) % 2))
        if turn == 0:
            prepare()
        if part == 0 and step >= 1:
            each_of_step(
                step, lambda o, side: over_known(step - 1, lambda other: attend_both(o, other))
            )

        def meet(origin, side):
            for hop in range(1, n_blk):
                kv_arrival(origin, part, hop)
            if turn < 2 * chain - 1:
                over_known(step, lambda other: attend(other, origin, part))

        each_of_step(step, meet)

    final = final_ref[:, pl.ds(pl.multiple_of(seq * width, width), width)]

    def vel_copy(target_z, target_core):
        target = target_z * 2 + target_core
        return pltpu.make_async_remote_copy(
            src_ref=vel_out.at[target],
            dst_ref=vel_in.at[seq],
            send_sem=vel_send.at[target],
            recv_sem=vel_recv.at[seq],
            device_id=(target, blk),
            device_id_type=MESH,
        )

    for turn in range(chain):
        q_pair = lax.rem(z + 1 + turn, chain)
        pl.when((z == 0) | (z == chain - 1))(lambda: attend(q_pair, chain - 1 - z, 1))
        attended = []
        for head in range(heads):
            total = acc_all[q_pair, head]
            attended.append((total[:, :HEAD_DIM] / total[:, HEAD_DIM:]).astype(BF16))
        attended = jnp.concatenate(attended, axis=1)
        for side in range(2):
            own = [
                attended[part * rows + side * half : part * rows + (side + 1) * half]
                for part in range(2)
            ]
            vel_out[q_pair * 2 + side] = nt_dot(final, jnp.concatenate(own, axis=0)).astype(BF16)
        if turn < chain - 1:
            for side in range(2):
                vel_copy(q_pair, side).start()
        else:
            vel_copy(z, 1 - core).start()
    vel_in[seq] = vel_out[seq]

    def vel_arrival(hop, carry):
        source = lax.rem(seq + hop, n_seq)
        pltpu.make_async_remote_copy(
            src_ref=vel_out.at[source],
            dst_ref=vel_in.at[source],
            send_sem=vel_send.at[source],
            recv_sem=vel_recv.at[source],
            device_id=(source, blk),
            device_id_type=MESH,
        ).wait_recv()
        return carry

    lax.fori_loop(1, n_seq, vel_arrival, 0)
    velocity = vel_in[0].astype(F32)
    for source in range(1, n_seq):
        velocity = velocity + vel_in[source].astype(F32)
    patch = noisy_ref.shape[0]
    latent = ((noisy_ref[...] - step_size * velocity) / scale_factor).astype(BF16)
    channel = lax.broadcasted_iota(jnp.int32, (LATENT_CH, patch), 0)
    feature = lax.broadcasted_iota(jnp.int32, (LATENT_CH, patch), 1)
    tile = jnp.zeros((LATENT_CH, TILE_VOX), F32)
    for sub in range(4):
        pick = jnp.where(feature == channel * 4 + sub, 1.0, 0.0).astype(BF16)
        tile = tile + jnp.dot(
            jnp.dot(pick, latent, preferred_element_type=F32).astype(BF16),
            spread[sub],
            preferred_element_type=F32,
        )
    own_tile[...] = tile.astype(BF16)

    n_same = chain * n_blk
    index = z * n_blk + blk
    keep = pltpu.make_async_copy(own_tile, tiles_ref.at[z, core, blk], local_sem.at[0])
    keep.start()

    def tile_copy(hop):
        other = lax.rem(index + hop, n_same)
        return pltpu.make_async_remote_copy(
            src_ref=own_tile,
            dst_ref=tiles_ref.at[z, core, blk],
            send_sem=tile_send.at[hop],
            recv_sem=tile_recv.at[index],
            device_id=(lax.div(other, n_blk) * 2 + core, lax.rem(other, n_blk)),
            device_id_type=MESH,
        )

    def tile_start(hop, carry):
        tile_copy(hop).start()
        return carry

    def tile_arrival(hop, carry):
        source = lax.rem(index + n_same - hop, n_same)
        pltpu.make_async_remote_copy(
            src_ref=own_tile,
            dst_ref=tiles_ref.at[lax.div(source, n_blk), core, lax.rem(source, n_blk)],
            send_sem=tile_send.at[hop],
            recv_sem=tile_recv.at[source],
            device_id=(lax.div(source, n_blk) * 2 + core, lax.rem(source, n_blk)),
            device_id_type=MESH,
        ).wait_recv()
        return carry

    def over_copy(source, from_own):
        slot = tiles_ref.at[lax.div(source, n_blk), core, lax.rem(source, n_blk)]
        return pltpu.make_async_remote_copy(
            src_ref=own_tile if from_own else slot,
            dst_ref=slot,
            send_sem=over_send.at[source],
            recv_sem=over_recv.at[source],
            device_id=(z * 2 + 1 - core, blk),
            device_id_type=MESH,
        )

    def tile_over(hop, carry):
        tile_arrival(hop, carry)
        over_copy(lax.rem(index + n_same - hop, n_same), False).start()
        return carry

    def over_arrival(source, carry):
        slot = tiles_ref.at[lax.div(source, n_blk), 1 - core, lax.rem(source, n_blk)]
        pltpu.make_async_remote_copy(
            src_ref=slot,
            dst_ref=slot,
            send_sem=over_send.at[source],
            recv_sem=over_recv.at[source],
            device_id=(z * 2 + 1 - core, blk),
            device_id_type=MESH,
        ).wait_recv()
        return carry

    lax.fori_loop(1, n_same, tile_start, 0)
    over_copy(index, True).start()

    for part in range(2):
        pl.when(z > 0)(lambda: go_left(None, part).wait_send())
        pl.when(z < chain - 1)(lambda: go_right(None, part).wait_send())
        go_over(None, part).wait_send()

        def settle(origin, side):
            if side == "left":
                pl.when(z < chain - 1)(lambda: go_right(origin, part).wait_send())
            else:
                pl.when(z > 0)(lambda: go_left(origin, part).wait_send())
            go_over(origin, part).wait_send()

        for step in range(1, chain):
            each_of_step(step, settle)

    def settle_kv(origin, carry):
        for part in range(2):
            for hop in range(1, n_blk):
                kv_copy(origin, part, hop).wait_send()
        return carry

    lax.fori_loop(0, chain, settle_kv, 0)
    for copy in keeps:
        copy.wait()

    def settle_vel(hop, carry):
        other = lax.rem(seq + hop, n_seq)
        vel_copy(lax.div(other, 2), lax.rem(other, 2)).wait_send()
        return carry

    lax.fori_loop(1, n_seq, settle_vel, 0)

    keep.wait()
    lax.fori_loop(1, n_same, tile_over, 0)

    def settle_tile(hop, carry):
        tile_copy(hop).wait_send()
        over_copy(lax.rem(index + n_same - hop, n_same), False).wait_send()
        return carry

    lax.fori_loop(1, n_same, settle_tile, 0)
    over_copy(index, True).wait_send()
    lax.fori_loop(0, n_same, over_arrival, 0)


def latent_tiles(
    n_seq, n_blk, tokens, project_weight, noisy_latent, final_weight, conv_weight, gain, shift
):
    chain = n_seq // 2
    rows, depth = tokens.shape
    width = project_weight.shape[2]
    channels = conv_weight.shape[1]
    heads = width // HEAD_DIM
    pair = 2 * rows
    dma = pltpu.SemaphoreType.DMA
    vmem = pl.BlockSpec(memory_space=pltpu.VMEM)
    hbm = pl.BlockSpec(memory_space=pl.ANY)
    kept = [
        ((channels, TAPS), BF16),
        ((channels, 2 * TAPS), BF16),
        ((channels, 128), F32),
        ((TILE_VOX, TILE_VOX), BF16),
    ]
    return pl.pallas_call(
        functools.partial(attention_kernel, chain, n_blk),
        out_shape=[jax.ShapeDtypeStruct((chain, 2, n_blk, LATENT_CH, TILE_VOX), BF16)]
        + [jax.ShapeDtypeStruct(*one) for one in kept],
        in_specs=[hbm, hbm] + [vmem] * 5,
        out_specs=[hbm] * 5,
        scratch_shapes=[
            pltpu.VMEM((chain, 2, 2, rows // 2, depth), BF16),
            pltpu.VMEM(project_weight.shape, BF16),
            pltpu.VMEM((chain, pair, width), BF16),
            pltpu.VMEM((chain, 2, 2, n_blk * rows, width), BF16),
            pltpu.VMEM((chain, heads, pair, 2 * HEAD_DIM), F32),
            pltpu.VMEM((chain, heads, pair, HEAD_DIM), F32),
            pltpu.VMEM((n_seq, noisy_latent.shape[0], rows), BF16),
            pltpu.VMEM((n_seq, noisy_latent.shape[0], rows), BF16),
            pltpu.VMEM((LATENT_CH, TILE_VOX), BF16),
            pltpu.VMEM((4, rows, TILE_VOX), BF16),
        ]
        + [pltpu.VMEM(*one) for one in kept]
        + [
            dma((3,)),
            dma((4,)),
            dma((chain, 2, 3)),
            dma((chain, 2, 2)),
            dma((chain, 2, n_blk)),
            dma((chain, 2, n_blk)),
            dma((n_seq,)),
            dma((n_seq,)),
            dma((chain * n_blk,)),
            dma((chain * n_blk,)),
            dma((chain * n_blk,)),
            dma((chain * n_blk,)),
        ],
        compiler_params=pltpu.CompilerParams(
            collective_id=0, has_side_effects=True, vmem_limit_bytes=60 * 2**20
        ),
        name="attention_to_tiles",
    )(tokens, project_weight, noisy_latent, final_weight, conv_weight, gain, shift)


def decode_kernel(
    n_blk,
    count_ref,
    inter_ref,
    tiles_ref,
    weight_first,
    weight_second,
    affine,
    place,
    out_ref,
    patches,
    upper_early,
    upper_late,
    lower_early,
    lower_late,
):
    slot = pl.program_id(0)
    rank = lax.axis_index("seq") * n_blk + lax.axis_index("blk")
    channels = weight_first.shape[0]
    some_ch = channels // 2
    group = channels // GROUPS
    half_vox = TILE_VOX // TILE_F
    inv = 1.0 / (group * TILE_F * FRAME)

    def gather():
        first = lax.fori_loop(0, rank, lambda i, total: total + count_ref[i], 0)
        stack = []
        for number in range(MAXPIX):
            pixel = jnp.minimum(first + number, inter_ref.shape[1] - 1)
            pieces = [tiles_ref[inter_ref[k, pixel]] for k in range(4)]
            for side in range(2):
                for frame in range(TILE_F):
                    lanes = slice(frame * half_vox, (frame + 1) * half_vox)
                    stack.append(
                        jnp.concatenate(
                            [pieces[2 * side][:, lanes], pieces[2 * side + 1][:, lanes]], axis=1
                        )
                    )
        strips = jnp.dot(jnp.concatenate(stack, axis=0), place[...], preferred_element_type=F32)
        held = TILE_F * LATENT_CH
        for number in range(MAXPIX):
            base = number * 2 * held
            region = jnp.concatenate(
                [strips[base : base + held], strips[base + held : base + 2 * held]], axis=1
            )
            lane = lax.broadcasted_iota(jnp.int32, region.shape, 1)
            column = lane & (REGION_COLS - 1)
            row = lane >> 5
            by_row = [
                jnp.where(row == 0, region, pltpu.roll(region, REGION_COLS, 1)),
                region,
                jnp.where(
                    row == REGION_ROWS - 1, region, pltpu.roll(region, FRAME - REGION_COLS, 1)
                ),
            ]
            for b in range(3):
                moved = by_row[b]
                by_col = [
                    jnp.where(column == 0, moved, pltpu.roll(moved, 1, 1)),
                    moved,
                    jnp.where(column == REGION_COLS - 1, moved, pltpu.roll(moved, FRAME - 1, 1)),
                ]
                for g in range(3):
                    tap = by_col[g].astype(BF16)
                    for frame in range(TILE_F):
                        start = frame * TAPS + (b * 3 + g) * LATENT_CH
                        patches[number, pl.ds(start, LATENT_CH), :] = tap[
                            frame * LATENT_CH : (frame + 1) * LATENT_CH
                        ]

    def convolve(number, side, early, late):
        some = pl.ds(side * some_ch, some_ch)
        early[...] = jnp.dot(
            weight_first[some, :], patches[number, :TAPS, :], preferred_element_type=F32
        )
        late[...] = jnp.dot(weight_second[some, :], patches[number], preferred_element_type=F32)

    def finish(side, early, late):
        parts = [x[...].reshape(some_ch // group, group, FRAME) for x in (early, late)]
        mean = jnp.sum(parts[0] + parts[1], axis=(1, 2), keepdims=True) * inv
        spread = jnp.square(parts[0] - mean) + jnp.square(parts[1] - mean)
        var = jnp.sum(spread, axis=(1, 2), keepdims=True) * inv
        both = affine[pl.ds(side * some_ch, some_ch), :]
        gain = both[:, 0:1].reshape(some_ch // group, group, 1)
        shift = both[:, 1:2].reshape(some_ch // group, group, 1)
        slope = 0.5 * gain * lax.rsqrt(var + norm_eps)
        offset = 0.5 * shift - mean * slope
        filled = slot < count_ref[rank]
        slope = jnp.where(filled, slope, 0.0)
        offset = jnp.where(filled, offset, 0.0)
        for frame in range(TILE_F):
            half = parts[frame] * slope + offset
            value = half + half * jnp.tanh(half)
            out_ref[0, 0, pl.ds(side * some_ch, some_ch), pl.ds(frame * FRAME, FRAME)] = (
                value.reshape(some_ch, FRAME).astype(BF16)
            )

    @pl.when(slot == 0)
    def begin():
        gather()
        convolve(0, 0, upper_early, upper_late)

    convolve(slot, 1, lower_early, lower_late)
    finish(0, upper_early, upper_late)
    convolve(jnp.minimum(slot + 1, MAXPIX - 1), 0, upper_early, upper_late)
    finish(1, lower_early, lower_late)


def decode(n_blk, tiles, prepared, owner_count, intersection):
    channels = prepared[0].shape[0]
    voxels = TILE_F * FRAME
    whole = lambda x: pl.BlockSpec(x.shape, lambda i, *_: (0,) * x.ndim)
    return pl.pallas_call(
        functools.partial(decode_kernel, n_blk),
        out_shape=jax.ShapeDtypeStruct((1, MAXPIX, channels, voxels), BF16),
        grid_spec=pltpu.PrefetchScalarGridSpec(
            num_scalar_prefetch=2,
            grid=(MAXPIX,),
            in_specs=[whole(tiles)] + [whole(x) for x in prepared],
            out_specs=pl.BlockSpec((1, 1, channels, voxels), lambda i, *_: (0, i, 0, 0)),
            scratch_shapes=[pltpu.VMEM((MAXPIX, 2 * TAPS, FRAME), BF16)]
            + [pltpu.VMEM((channels // 2, FRAME), F32)] * 4,
        ),
        compiler_params=pltpu.CompilerParams(vmem_limit_bytes=60 * 2**20),
        name="decode_tiles",
    )(owner_count, intersection.T, tiles, *prepared)


def body(
    n_seq,
    n_blk,
    tokens,
    project_weight,
    noisy_latent,
    final_weight,
    conv_weight,
    norm_gain,
    norm_shift,
    owner_count,
    intersection,
):
    tiles, *prepared = latent_tiles(
        n_seq,
        n_blk,
        tokens,
        project_weight,
        noisy_latent.T,
        final_weight.T,
        conv_weight,
        norm_gain.reshape(1, -1),
        norm_shift.reshape(1, -1),
    )
    tiles = tiles.reshape(-1, LATENT_CH, TILE_VOX)
    return decode(n_blk, tiles, prepared, owner_count, intersection)


def solution(mesh):
    return jax.shard_map(
        functools.partial(body, mesh.shape["seq"], mesh.shape["blk"]),
        mesh=mesh,
        in_specs=(
            P(("seq", "blk"), None),
            P(None, None, "seq"),
            P(("seq", "blk"), None),
            P(),
            P(),
            P(),
            P(),
            P(),
            P(),
        ),
        out_specs=P(("seq", "blk"), None, None, None),
        check_vma=False,
    )
```
